256 devices in a mesh: ctx: 32 (over x_hi, z, core), fsdp: 8 (over x_lo, y).
Axes of the slice: x: 4 (x_hi: 2, x_lo: 2; x = x_hi * 2 + x_lo), y: 4, z: 8, core: 2. Of those that a mesh axis runs over, the one named last changes fastest.
Arguments:
- hidden_states: bfloat16 [12288, 8192], P('ctx', 'fsdp'), may hold values from -6 to 6
- norm_gain: bfloat16 [8192], replicated, may hold values from 0.25 to 1.75
- qkv_weight: bfloat16 [8192, 8, 1280], P('ctx', 'fsdp')
- block_mask: int32 [64, 8, 10], P('ctx', 'fsdp'), may hold values 0 or 1
Outputs:
- attended: bfloat16 [12288, 8, 1024], P('ctx', 'fsdp')
The draws below stay inside these ranges and needn't reach their ends.
All inputs are finite; a program needn't handle non-finite values. No bound on the sum of `block_mask` on one device may be relied on, other than what follows from the above.
Results may differ from the reference program's by a relative error of at most 0.008.
The reference program's roundings to bfloat16 on the way (of `normed`, `masked`, `queries`, `key_rows`, `value_rows` and `probs`) count: a program that leaves them out, or rounds other values in their place, can miss the bound.
Values may be sent and summed in bfloat16 or wider, within the bound.
A program may use at most 128 MiB of HBM per device.

```python
import math
import jax
import jax.numpy as jnp
from jax import lax

D = 8192
KVH = 8
HD = 128
TOK_DEV = 384
STEPS = 4
RB = 128
QPG = 8
SEQ = 12288
N_CTX = 32


def draw_qkv_weight(key, part):
    first_key = jax.random.fold_in(jax.random.fold_in(key, 17), 0)
    dimensions = (D, KVH, (QPG + 2) * HD)
    entries = jnp.clip(jax.random.normal(first_key, dimensions, jnp.float32), -6.0, 6.0)
    return (entries * (1.7 / math.sqrt(D))).astype(jnp.bfloat16)


def plant(values, rng, smallest, high):
    dims = values.shape
    index_at = [jax.random.randint(jax.random.fold_in(rng, axis), (), 0, dims[axis]) for axis in range(len(dims))]
    values = values.at[tuple(index_at)].set(smallest)
    longest = dims.index(max(dims))
    index_at[longest] = (index_at[longest] + 1) % dims[longest]
    return values.at[tuple(index_at)].set(high)


def shard_levels(key, extent, cuts, least, high):
    factor_of = 1.0
    for axis_at, blocks in cuts:
        draws = jax.random.uniform(jax.random.fold_in(jax.random.fold_in(key, 6), axis_at), (blocks,), jnp.float32, least / len(cuts), high / len(cuts))
        factor_of = factor_of * jnp.repeat(jnp.exp(draws), extent[axis_at] // blocks).reshape((-1,) + (1,) * (len(extent) - 1 - axis_at))
    return factor_of


def centred(stream_key, extent, spread, most, cuts=(), held_as=jnp.bfloat16):
    values = spread * jax.random.normal(stream_key, extent, jnp.float32)
    if cuts:
        values = values * shard_levels(stream_key, extent, cuts, -0.22, 0.18)
    return jnp.clip(values, -most, most).astype(held_as)


def setup_inputs(seed: int = 0) -> dict:
    key_list = jax.random.split(jax.random.key(seed), 5)
    hidden_states = centred(key_list[0], (SEQ, D), 1.0, 6.0, ((0, 32), (1, 8)))
    norm_gain = jnp.clip(1.0 + 0.15 * jax.random.normal(key_list[1], (D,), jnp.float32), 0.25, 1.75).astype(jnp.bfloat16)
    qkv_weight = draw_qkv_weight(jax.random.fold_in(key_list[4], 71), 0)
    block_mask = plant((jax.random.randint(key_list[3], (D // RB, KVH, QPG + 2), 0, 4) < 3).astype(jnp.int32), jax.random.fold_in(key_list[3], 1), 0, 1)
    return {"hidden_states": hidden_states, "norm_gain": norm_gain, "qkv_weight": qkv_weight, "block_mask": block_mask}


def rotary(values, position):
    halfway = values.shape[-1] // 2
    exponent = jnp.arange(0, 2 * halfway, 2).astype(jnp.float32) / (2 * halfway)
    inverse = jnp.power(jnp.float32(500000.0), -exponent)
    angles = position[:, None] * inverse[None, :]
    target = (angles.shape[0],) + (1,) * (values.ndim - 2) + (halfway,)
    cosine = jnp.cos(angles).reshape(target)
    sine_term = jnp.sin(angles).reshape(target)
    leading = values[..., :halfway]
    trailing = values[..., halfway:]
    return jnp.concatenate([leading * cosine - trailing * sine_term, trailing * cosine + leading * sine_term], axis=-1)

def attend(queries, key_rows, value_rows, query_start, key_start, window):
    scores = jnp.einsum('tgqd,kgd->gqtk', queries, key_rows, preferred_element_type=jnp.float32) * HD ** (-0.5)
    query_position = query_start + jnp.arange(queries.shape[0], dtype=jnp.int32)
    key_position = key_start + jnp.arange(key_rows.shape[0], dtype=jnp.int32)
    allowed = (key_position[None, :] <= query_position[:, None]) & (key_position[None, :] > query_position[:, None] - window) & (key_position[None, :] >= 0)
    scores = jnp.where(allowed[None, None], scores, -1e+30)
    row_peak = lax.optimization_barrier(jnp.max(scores, axis=-1, keepdims=True))
    exponent = jnp.exp(scores - row_peak)
    row_total = lax.optimization_barrier(jnp.sum(exponent, axis=-1, keepdims=True))
    probs = (exponent / row_total).astype(jnp.bfloat16)
    probs_wide = lax.optimization_barrier(probs).astype(jnp.float32)
    output = jnp.einsum('gqtk,kgd->tgqd', probs_wide, value_rows, preferred_element_type=jnp.float32)
    return output.astype(jnp.bfloat16).reshape(queries.shape[0], queries.shape[1], queries.shape[2] * queries.shape[3])

def reference(hidden_states, norm_gain, qkv_weight, block_mask):
    states = hidden_states.astype(jnp.float32)
    mean_square = lax.optimization_barrier(jnp.mean(states * states, axis=1, keepdims=True))
    normed = (states * lax.rsqrt(mean_square + 1e-05) * norm_gain.astype(jnp.float32)[None, :]).astype(jnp.bfloat16)
    shaped = qkv_weight.reshape(D // RB, RB, KVH, QPG + 2, HD)
    masked = (shaped * block_mask.astype(jnp.bfloat16)[:, None, :, :, None]).reshape(D, KVH * (QPG + 2) * HD)
    projected = jnp.dot(normed, masked, preferred_element_type=jnp.float32).reshape(SEQ, KVH, (QPG + 2) * HD)
    position = jnp.arange(SEQ, dtype=jnp.int32).astype(jnp.float32)
    queries = rotary(projected[..., :QPG * HD].reshape(SEQ, KVH, QPG, HD), position).astype(jnp.bfloat16)
    key_rows = rotary(projected[..., QPG * HD:(QPG + 1) * HD], position).astype(jnp.bfloat16)
    value_rows = projected[..., (QPG + 1) * HD:].astype(jnp.bfloat16)
    queries, key_rows, value_rows = lax.optimization_barrier((queries, key_rows, value_rows))
    padding = jnp.zeros((STEPS * TOK_DEV, KVH, HD), jnp.bfloat16)
    padded_keys = jnp.concatenate([padding, key_rows], axis=0)
    padded_values = jnp.concatenate([padding, value_rows], axis=0)

    def one_block(block_index):
        first_row = block_index * TOK_DEV
        query_block = lax.dynamic_slice_in_dim(queries, first_row, TOK_DEV, 0).astype(jnp.float32)
        key_block = lax.dynamic_slice_in_dim(padded_keys, first_row, (STEPS + 1) * TOK_DEV, 0).astype(jnp.float32)
        value_block = lax.dynamic_slice_in_dim(padded_values, first_row, (STEPS + 1) * TOK_DEV, 0).astype(jnp.float32)
        return attend(query_block, key_block, value_block, first_row, first_row - STEPS * TOK_DEV, STEPS * TOK_DEV)
    blocks = lax.map(one_block, jnp.arange(N_CTX, dtype=jnp.int32))
    return blocks.reshape(SEQ, KVH, QPG * HD)
```

```python
import jax
import jax.numpy as jnp
from jax import lax
from jax.experimental import pallas as pl
from jax.experimental.pallas import tpu as pltpu
from jax.sharding import PartitionSpec as P

MESH = pl.DeviceIdType.MESH
F32 = jnp.float32
BF16 = jnp.bfloat16
HD = 128
TOK = 384
WID = 1024
KH = 4096
ROWS = 256
NCH = 5
SUB = 48
NSUB = TOK // SUB
HALF = TOK // 2
STEPS = 4
WIN = STEPS * TOK + HD
NEG = -1e30
EXP_SCALE = HD ** (-0.5) * 1.4426950408889634


class Plan:
    def __init__(self):
        self.tasks = []
        self.waits = {}

    def token(self, name, wait=None):
        self.waits[name] = wait
        return name

    def add(self, name, deps, dur, prio, emit, sends=()):
        self.tasks.append((name, list(deps), dur, prio, emit, list(sends)))

    def order(self, start):
        ready = {name: 0.0 for name in start}
        free = {}
        now = 0.0
        left = list(self.tasks)
        done = []
        while left:
            best = None
            soonest = None
            for task in left:
                if all(d in ready for d in task[1]):
                    at = max([ready[d] for d in task[1]], default=0.0)
                    if at <= now:
                        if best is None or task[3] < best[3]:
                            best = task
                    elif soonest is None or at < soonest:
                        soonest = at
            if best is None:
                now = soonest
                continue
            left.remove(best)
            done.append(best)
            now += best[2]
            ready["done:" + best[0]] = now
            for link, dur, lat, token in best[5]:
                begin = max(now, free.get(link, 0.0))
                free[link] = begin + dur
                ready[token] = begin + dur + lat
        self.total = now
        return done

    def emit(self, start):
        waited = set()
        for name, deps, _, _, emit, _ in self.order(start):
            for d in deps:
                if d not in waited and self.waits.get(d) is not None:
                    self.waits[d]()
                waited.add(d)
            emit()


def body(
    x_hbm, g_ref, w_hbm, mask_ref, cos_hbm, sin_hbm, o_hbm,
    xv, wv, cosv, sinv, hid, nrm, wts, part, got, acc, qbuf, kvb, out, sq, tot, rs,
    in_s, wz_s, wz_r, ws_s, ws_r, hx_s, hx_r, hy_s, hy_r, sq_s, sq_r, tx_s, tx_r,
    pr_s, pr_r, kv_s, kv_r, o_s,
):
    ci = lax.axis_index("ctx")
    fi = lax.axis_index("fsdp")
    xh, z, c = ci // 16, (ci // 2) % 8, ci % 2
    xl, y = fi // 4, fi % 4
    inner = xh != xl

    def dev(xh_, z_, c_, xl_, y_):
        return (xh_ * 16 + z_ * 2 + c_, xl_ * 4 + y_)

    up = dev(xh, (z + 1) % 8, c, xl, y)
    down = dev(xh, (z + 7) % 8, c, xl, y)
    sib = dev(xh, z, 1 - c, xl, y)
    far = dev(1 - xh, z, c, xl, y)
    cross = dev(1 - xh, z, c, 1 - xl, y)
    side = dev(xh, z, c, 1 - xl, y)
    yup = dev(xh, z, c, xl, (y + 1) % 4)
    ydown = dev(xh, z, c, xl, (y + 3) % 4)
    after = ((ci + 2) % 32, fi)
    before = ((ci + 30) % 32, fi)
    peers = [(ci, (fi + k) % 8) for k in range(1, 8)]

    started = []

    def remote(src, dst, s, r, to):
        return pltpu.make_async_remote_copy(
            src_ref=src, dst_ref=dst, send_sem=s, recv_sem=r, device_id=to, device_id_type=MESH
        )

    def send(*args):
        cp = remote(*args)
        cp.start()
        started.append(cp)

    load_w = pltpu.make_async_copy(w_hbm, wv, in_s.at[0])
    load_x = pltpu.make_async_copy(x_hbm, xv, in_s.at[1])
    load_c = pltpu.make_async_copy(cos_hbm, cosv, in_s.at[2])
    load_n = pltpu.make_async_copy(sin_hbm, sinv, in_s.at[3])
    load_h = pltpu.make_async_copy(x_hbm, hid.at[1, y], in_s.at[4])
    load_w.start()
    load_x.start()
    load_c.start()
    load_n.start()

    @pl.when(jnp.logical_not(inner))
    def _():
        load_h.start()

    barrier = pltpu.get_barrier_semaphore()
    greeted = peers + [far, cross, up, down, sib, after, before]
    for d in greeted:
        pl.semaphore_signal(barrier, inc=1, device_id=d, device_id_type=MESH)

    load_w.wait()
    own_piece = z * 2 + c

    def piece(j, idx):
        return wts.at[j, pl.ds(pl.multiple_of(idx * ROWS, ROWS), ROWS)]

    for j in range(NCH):
        for half in range(2):
            head = 8 + half if j == 0 else 2 * (j - 1) + half
            for rb in range(2):
                keep = mask_ref[rb, head].astype(F32)
                block = wv[rb * 128:(rb + 1) * 128, head * 128:(head + 1) * 128].astype(F32)
                wts[j, pl.ds(pl.multiple_of(own_piece * ROWS + rb * 128, 128), 128), half * 128:(half + 1) * 128] = (
                    block * keep
                ).astype(BF16)
    load_x.wait()
    pl.semaphore_wait(barrier, len(greeted))

    def hrows(m):
        return pl.ds(m * SUB, SUB)

    first_to = (
        jnp.where(inner, cross[0], side[0]),
        jnp.where(inner, cross[1], side[1]),
    )
    first_t = jnp.where(inner, 0, 1)

    def first_send(m):
        send(xv.at[hrows(m)], hid.at[first_t, y, hrows(m)], hx_s.at[0, m], hx_r.at[first_t, m], first_to)

    def own_send(j):
        src = piece(j, own_piece)
        send(src, src, wz_s.at[j, 0, 0], wz_r.at[j, 0, 0], up)
        send(src, src, wz_s.at[j, 1, 0], wz_r.at[j, 1, 0], down)
        send(src, src, ws_s.at[j, 0], ws_r.at[j, 0], sib)

    first_send(0)
    own_send(0)
    first_send(1)
    own_send(1)
    for m in range(2, NSUB):
        first_send(m)

    @pl.when(jnp.logical_not(inner))
    def _():
        load_h.wait()

    lanes = jnp.zeros((TOK, 128), F32)
    for k in range(WID // 128):
        v = xv[:, k * 128:(k + 1) * 128].astype(F32)
        lanes = lanes + v * v
    sums = lax.dot_general(
        jnp.ones((8, 128), F32), lanes, (((1,), (1,)), ((), ())),
        precision=lax.Precision.HIGHEST, preferred_element_type=F32,
    )
    sq[fi] = sums
    for k in range(1, 8):
        send(sq.at[fi], sq.at[fi], sq_s.at[k - 1], sq_r.at[k - 1], peers[k - 1])

    plan = Plan()
    start = []

    def at(step):
        return ((z + 8 + step) % 8) * 2 + c

    pz, lz = 2.9, 1.5

    def wait_w(j, way, d):
        def go():
            if d < 3:
                ref = piece(j, at(-(d + 1) if way == 0 else d + 1))
            else:
                ref = wts.at[j, pl.ds(pl.multiple_of(at(4) * ROWS + way * 128, 128), 128)]
            remote(ref, ref, wz_s.at[j, way, d], wz_r.at[j, way, d], sib).wait_recv()
        return go

    def wait_s(j, k):
        def go():
            ref = wts.at[j, pl.ds(0, ROWS)]
            remote(ref, ref, ws_s.at[j, k], ws_r.at[j, k], sib).wait_recv()
        return go

    for j in range(NCH):
        for way in range(2):
            for d in range(4):
                plan.token(f"w{j}{way}{d}", wait_w(j, way, d))
        for k in range(8):
            plan.token(f"s{j}{k}", wait_s(j, k))

    def own_task(j):
        plan.add(
            f"own{j}", [f"done:w{j-2}02f", f"done:w{j-2}12f"] if j >= 2 else [], 0.3, 0,
            (lambda: own_send(j)) if j >= 2 else (lambda: None),
            [("zu", pz, lz, f"w{j}00"), ("zd", pz, lz, f"w{j}10"), ("cc", 0.6, 1.0, f"s{j}0")],
        )

    def fwd_task(j, way, d):
        def go():
            idx = at(-(d + 1) if way == 0 else d + 1)
            to = up if way == 0 else down
            if d < 2:
                src = piece(j, idx)
            else:
                src = wts.at[j, pl.ds(pl.multiple_of(idx * ROWS + way * 128, 128), 128)]
            send(src, src, wz_s.at[j, way, d + 1], wz_r.at[j, way, d + 1], to)
            src = piece(j, idx)
            k = 1 + way * 3 + d
            send(src, src, ws_s.at[j, k], ws_r.at[j, k], sib)
        link = "zu" if way == 0 else "zd"
        plan.add(
            f"w{j}{way}{d}f", [f"w{j}{way}{d}"], 0.2, 1, go,
            [(link, pz if d < 2 else pz / 2, lz, f"w{j}{way}{d+1}"), ("cc", 0.6, 1.0, f"s{j}{1+way*3+d}")],
        )

    def last_task(j):
        def go():
            src = piece(j, at(4))
            send(src, src, ws_s.at[j, 7], ws_r.at[j, 7], sib)
        plan.add(f"w{j}l", [f"w{j}03", f"w{j}13"], 0.1, 1, go, [("cc", 0.6, 1.0, f"s{j}7")])

    for j in range(NCH):
        own_task(j)
        for way in range(2):
            for d in range(3):
                fwd_task(j, way, d)
        last_task(j)
    chunk_in = [
        [f"s{j}{k}" for k in range(8)]
        + [f"done:w{j}{way}{d}f" for way in range(2) for d in range(3)]
        + [f"done:w{j}l"]
        for j in range(NCH)
    ]

    ph, lh = 2.2, 1.5

    def hpiece(t, yy, m):
        return hid.at[t, yy, hrows(m)]

    def wait_hx(t, m):
        ref = hpiece(t, y, m)
        remote(ref, ref, hx_s.at[0, m], hx_r.at[t, m], sib).wait_recv()

    def y_sends(t, m):
        ref = hpiece(t, y, m)
        send_when.append(remote(ref, ref, hy_s.at[t, m, 0], hy_r.at[t, m, 0], yup))
        send_when[-1].start()
        send_when.append(remote(ref, ref, hy_s.at[t, m, 1], hy_r.at[t, m, 1], ydown))
        send_when[-1].start()

    send_when = []
    y_links = lambda t, m: [("yu", ph, lh, f"y{t}{m}0"), ("yd", ph, lh, f"y{t}{m}1")]
    seq = [(1, 0), (0, 0), (1, 1), (0, 1)] + [(0, m) for m in range(2, NSUB)] + [(1, m) for m in range(2, NSUB)]
    rank = {tm: n for n, tm in enumerate(seq)}
    for m in range(NSUB):
        start.append(f"x1{m}")
        start.append(f"x0{m}")

    def x_in(m):
        def go():
            @pl.when(inner)
            def _():
                wait_hx(0, m)
                ref = hpiece(0, y, m)
                remote(ref, ref, hx_s.at[1, m], hx_r.at[0, m], side).start()
                y_sends(0, m)
        plan.add(f"xi0{m}", [f"xa0{m}"], 0.1, 2, go, [("xo", ph, lh, f"xb0{m}")])

    def x_out(m):
        def go():
            @pl.when(jnp.logical_not(inner))
            def _():
                wait_hx(0, m)
                y_sends(0, m)
        plan.add(f"xo0{m}", [f"xb0{m}"], 0.1, 2, go, y_links(0, m))

    def x_own(m):
        def go():
            @pl.when(inner)
            def _():
                wait_hx(1, m)
            y_sends(1, m)
        deps = [f"xc1{m}"] + ([f"done:xo0{NSUB-1}"] if m >= 2 else [])
        plan.add(f"xo1{m}", deps, 0.1, 3, go, y_links(1, m))

    plan.add(
        "first", [], 0.5, -1, lambda: None,
        [("xi", ph, lh, f"xa0{m}") for m in range(NSUB)] + [("xs", ph, lh, f"xc1{m}") for m in range(NSUB)],
    )
    for m in range(NSUB):
        x_in(m)
        x_out(m)
        x_own(m)

    def wait_y(t, m, k):
        def go():
            idx = (y + 3) % 4 if k == 0 else (y + 1) % 4 if k == 1 else (y + 2) % 4
            ref = hpiece(t, idx, m)
            remote(ref, ref, hy_s.at[t, m, k], hy_r.at[t, m, k], sib).wait_recv()
        return go

    def y_task(t, m):
        way = m % 2
        for k in range(3):
            plan.token(f"y{t}{m}{k}", wait_y(t, m, k))

        def go():
            ref = hpiece(t, (y + 3) % 4 if way == 0 else (y + 1) % 4, m)
            send(ref, ref, hy_s.at[t, m, 2], hy_r.at[t, m, 2], yup if way == 0 else ydown)
        plan.add(
            f"yf{t}{m}", [f"y{t}{m}{way}"], 0.1, 2, go, [("yu" if way == 0 else "yd", ph, lh, f"y{t}{m}2")]
        )

    def wait_sq(k):
        def go():
            remote(sq.at[0], sq.at[0], sq_s.at[k], sq_r.at[k], sib).wait_recv()
        return go

    def spread(which, rows8):
        inv = lax.rsqrt(rows8 * (1.0 / 8192.0) + 1e-05)
        rs[which] = lax.dot_general(
            inv, jnp.full((8, 128), 0.125, F32), (((0,), (0,)), ((), ())),
            precision=lax.Precision.HIGHEST, preferred_element_type=F32,
        )

    def total():
        rows8 = sq[0]
        for k in range(1, 8):
            rows8 = rows8 + sq[k]
        tot[1] = rows8
        send(tot.at[1], tot.at[0], tx_s.at[0], tx_r.at[0], far)
        spread(1, rows8)

    def wait_tx():
        remote(tot.at[1], tot.at[0], tx_s.at[0], tx_r.at[0], far).wait_recv()

    plan.token("tx", wait_tx)
    for k in range(7):
        start.append(plan.token(f"sq{k}", wait_sq(k)))
    plan.add("sqa", ["done:first"], 3.0, 0, lambda: None)
    plan.add("total", [f"sq{k}" for k in range(7)] + ["done:sqa"], 0.5, 1, total, [("none", 0, 2.5, "tx")])
    plan.add("other", ["tx"], 0.5, 1, lambda: spread(0, tot[0]))

    def norm_task(t, m, step, deps):
        def go():
            yy = (y + step) % 4
            gain = g_ref[pl.ds(xh * 4 + yy, 1), :]
            scale = rs[t, m * SUB:(m + 1) * SUB, :]
            for k in range(WID // 128):
                v = hid[t, yy, m * SUB:(m + 1) * SUB, k * 128:(k + 1) * 128].astype(F32)
                v = v * scale * gain[:, k * 128:(k + 1) * 128]
                nrm[t, m * SUB:(m + 1) * SUB, pl.ds(pl.multiple_of(yy * WID + k * 128, 128), 128)] = v.astype(BF16)
        plan.add(f"n{t}{m}{step}", deps + ["done:other" if t == 0 else "done:total"], 0.15, 4 + rank[(t, m)] * 0.01, go)

    for t in range(2):
        for m in range(NSUB):
            y_task(t, m)
            norm_task(t, m, 0, [f"done:xo{t}{m}"] + ([f"done:xi{t}{m}"] if t == 0 else []))
            norm_task(t, m, 3, [f"y{t}{m}0"])
            norm_task(t, m, 1, [f"y{t}{m}1"])
            norm_task(t, m, 2, [f"y{t}{m}2"])

    per_half = NSUB // 2

    def normed_in(t, h):
        return [f"done:n{t}{m}{s}" for m in range(h * per_half, (h + 1) * per_half) for s in range(4)]

    def product(t, h, j):
        return jnp.dot(nrm[t, h * HALF:(h + 1) * HALF, :], wts[j], preferred_element_type=F32)

    def wait_pr(j, h):
        def go():
            ref = got.at[j, pl.ds(h * HALF, HALF)]
            remote(ref, ref, pr_s.at[j, h], pr_r.at[j, h], far).wait_recv()
        return go

    def other_task(h, j):
        def go():
            rows = pl.ds(h * HALF, HALF)
            part[j, rows] = product(0, h, j)
            send(part.at[j, rows], got.at[j, rows], pr_s.at[j, h], pr_r.at[j, h], far)
        plan.token(f"p{j}{h}", wait_pr(j, h))
        plan.add(f"m0{h}{j}", normed_in(0, h) + chunk_in[j], 0.6, 5 + j * 0.1 + h * 0.01, go, [("xp", 4.4, 2.0, f"p{j}{h}")])

    def rotated(u, rows):
        return u * cosv[rows, :] + pltpu.roll(u, 64, 1) * sinv[rows, :]

    def own_product(h, j):
        def go():
            rows = pl.ds(h * HALF, HALF)
            acc[j, rows] = product(1, h, j)
        plan.add(f"m1{h}{j}", normed_in(1, h) + chunk_in[j], 0.6, 6 + j * 0.1 + h * 0.01, go)

    def kv_send(blk_from, blk_to, h, k, to):
        rows = pl.ds(h * HALF, HALF)
        send(kvb.at[blk_from, rows], kvb.at[blk_to, rows], kv_s.at[k, h], kv_r.at[k, h], to)

    def finish(h, j):
        def go():
            rows = pl.ds(h * HALF, HALF)
            u = acc[j, rows] + got[j, rows]
            left, right = u[:, :HD], u[:, HD:]
            if j == 0:
                kvb[4 + c, rows, 0:HD] = rotated(left, rows).astype(BF16)
                kvb[4 + c, rows, HD:2 * HD] = right.astype(BF16)
                kv_send(4 + c, 2 + c, h, 0, after)
                kv_send(4 + c, 4 + c, h, 2, sib)
            else:
                qbuf[j - 1, rows, 0:HD] = rotated(left, rows).astype(BF16)
                qbuf[j - 1, rows, HD:2 * HD] = rotated(right, rows).astype(BF16)
        sends = [("zu", 2.2, 2.0, f"k0{h}"), ("cc", 0.3, 1.0, f"k2{h}")] if j == 0 else []
        plan.add(f"f{h}{j}", [f"done:m1{h}{j}", f"p{j}{h}", "done:rope"], 0.3, 4.5 + j * 0.1, go, sends)

    def rope():
        load_c.wait()
        load_n.wait()

    plan.add("rope", [], 0.1, 20, rope)

    def wait_kv(k, h):
        def go():
            ref = kvb.at[0, pl.ds(0, HALF)]
            remote(ref, ref, kv_s.at[k, h], kv_r.at[k, h], sib).wait_recv()
        return go

    for h in range(2):
        for k in range(5):
            plan.token(f"k{k}{h}", wait_kv(k, h))

        def pass_one(h=h):
            kv_send(2 + c, c, h, 1, after)
            kv_send(2 + c, 2 + c, h, 3, sib)

        def pass_two(h=h):
            kv_send(c, c, h, 4, sib)

        plan.add(f"ka{h}", [f"k0{h}"], 0.1, 1, pass_one, [("zu", 2.2, 2.0, f"k1{h}"), ("cc", 0.3, 1.0, f"k3{h}")])
        plan.add(f"kb{h}", [f"k1{h}"], 0.1, 1, pass_two, [("cc", 0.3, 1.0, f"k4{h}")])
        for j in range(NCH):
            other_task(h, j)
            own_product(h, j)
            finish(h, j)
    window_in = [f"k{k}{h}" for k in (2, 3, 4) for h in range(2)] + [f"done:kb{h}" for h in range(2)] + [f"done:f{h}0" for h in range(2)]

    def attend(j):
        def go():
            row = lax.broadcasted_iota(jnp.int32, (HD, HD), 0)
            col = lax.broadcasted_iota(jnp.int32, (HD, HD), 1)
            later = col > row
            key_at = lax.broadcasted_iota(jnp.int32, (1, WIN), 1)

            def block(b, carry):
                r0 = pl.multiple_of(b * HD, HD)
                k0 = pl.multiple_of(c * TOK + b * HD, HD)
                keys = kvf[pl.ds(k0, WIN), 0:HD]
                vals = kvf[pl.ds(k0, WIN), HD:2 * HD]
                real = key_at >= (STEPS - ci) * TOK - b * HD
                for half in range(2):
                    q = qbuf[j - 1, pl.ds(r0, HD), half * HD:(half + 1) * HD]
                    s = lax.dot_general(q, keys, (((1,), (1,)), ((), ())), preferred_element_type=F32)
                    s = jnp.concatenate(
                        [
                            jnp.where(later, s[:, :HD], NEG),
                            s[:, HD:WIN - HD],
                            jnp.where(later, NEG, s[:, WIN - HD:]),
                        ],
                        axis=1,
                    )
                    s = jnp.where(real, s, NEG)
                    peak = jnp.max(s, axis=1, keepdims=True)
                    e = jnp.exp2((s - peak) * EXP_SCALE)
                    probs = (e * (1.0 / jnp.sum(e, axis=1, keepdims=True))).astype(BF16)
                    o = jnp.dot(probs, vals, preferred_element_type=F32)
                    out[j - 1, pl.ds(r0, HD), half * HD:(half + 1) * HD] = o.astype(BF16)
                return carry

            lax.fori_loop(0, TOK // HD, block, 0)
            pltpu.make_async_copy(out.at[j - 1], o_hbm.at[:, pl.ds((j - 1) * 256, 256)], o_s.at[j - 1]).start()
        plan.add(f"a{j}", window_in + [f"done:f{h}{j}" for h in range(2)], 3.0, 7 + j, go)

    kvf = kvb.reshape(6 * TOK, 2 * HD)
    for j in range(1, NCH):
        attend(j)

    plan.emit(start)
    body.total = plan.total

    for j in range(1, NCH):
        pltpu.make_async_copy(out.at[j - 1], o_hbm.at[:, pl.ds((j - 1) * 256, 256)], o_s.at[j - 1]).wait()
    for cp in started:
        cp.wait_send()
    for t in range(2):
        for m in range(NSUB):
            for k in range(2):
                ref = hpiece(t, y, m)
                remote(ref, ref, hy_s.at[t, m, k], hy_r.at[t, m, k], yup).wait_send()

    @pl.when(inner)
    def _():
        for m in range(NSUB):
            ref = hpiece(0, y, m)
            remote(ref, ref, hx_s.at[1, m], hx_r.at[0, m], side).wait_send()


def shards(hidden_states, norm_gain, qkv_weight, block_mask):
    ci = lax.axis_index("ctx")
    position = (ci * TOK + jnp.arange(TOK, dtype=jnp.int32)).astype(F32)
    inverse = jnp.power(F32(500000.0), -(jnp.arange(0, HD, 2).astype(F32) / HD))
    angles = position[:, None] * inverse[None, :]
    cosine, sine = jnp.cos(angles), jnp.sin(angles)
    cos2 = jnp.concatenate([cosine, cosine], axis=1)
    sin2 = jnp.concatenate([-sine, sine], axis=1)
    gain = norm_gain.astype(F32).reshape(8, WID)
    any_ = pl.BlockSpec(memory_space=pl.ANY)
    dma = pltpu.SemaphoreType.DMA
    result = pl.pallas_call(
        body,
        out_shape=jax.ShapeDtypeStruct((TOK, 1024), BF16),
        in_specs=[
            any_, pl.BlockSpec(memory_space=pltpu.VMEM), any_, pl.BlockSpec(memory_space=pltpu.SMEM), any_, any_,
        ],
        out_specs=any_,
        scratch_shapes=[
            pltpu.VMEM((TOK, WID), BF16),
            pltpu.VMEM((ROWS, 1280), BF16),
            pltpu.VMEM((TOK, HD), F32),
            pltpu.VMEM((TOK, HD), F32),
            pltpu.VMEM((2, 4, TOK, WID), BF16),
            pltpu.VMEM((2, TOK, KH), BF16),
            pltpu.VMEM((NCH, KH, 256), BF16),
            pltpu.VMEM((NCH, TOK, 256), F32),
            pltpu.VMEM((NCH, TOK, 256), F32),
            pltpu.VMEM((NCH, TOK, 256), F32),
            pltpu.VMEM((4, TOK, 256), BF16),
            pltpu.VMEM((6, TOK, 256), BF16),
            pltpu.VMEM((4, TOK, 256), BF16),
            pltpu.VMEM((8, 8, TOK), F32),
            pltpu.VMEM((2, 8, TOK), F32),
            pltpu.VMEM((2, TOK, HD), F32),
            dma((5,)),
            dma((NCH, 2, 4)), dma((NCH, 2, 4)),
            dma((NCH, 8)), dma((NCH, 8)),
            dma((2, NSUB)), dma((2, NSUB)),
            dma((2, NSUB, 3)), dma((2, NSUB, 3)),
            dma((7,)), dma((7,)),
            dma((1,)), dma((1,)),
            dma((NCH, 2)), dma((NCH, 2)),
            dma((5, 2)), dma((5, 2)),
            dma((4,)),
        ],
        compiler_params=pltpu.CompilerParams(
            collective_id=0, has_side_effects=True, vmem_limit_bytes=58 * 2**20
        ),
        cost_estimate=pl.CostEstimate(flops=12 * 10**9, bytes_accessed=3 * 10**6, transcendentals=6 * 10**6),
    )(
        hidden_states, gain, qkv_weight.reshape(ROWS, 1280), block_mask.reshape(2, 10), cos2, sin2,
    )
    return result.reshape(TOK, 1, 1024)


def solution(mesh):
    return jax.shard_map(
        shards,
        mesh=mesh,
        in_specs=(P("ctx", "fsdp"), P(), P("ctx", "fsdp", None), P("ctx", "fsdp", None)),
        out_specs=P("ctx", "fsdp", None),
        check_vma=False,
    )
```

```python
import jax
import jax.numpy as jnp
from jax import lax
from jax.experimental import pallas as pl
from jax.experimental.pallas import tpu as pltpu
from jax.sharding import PartitionSpec as P

MESH = pl.DeviceIdType.MESH
F32 = jnp.float32
BF16 = jnp.bfloat16
HD = 128
TOK = 384
WID = 1024
KH = 4096
ROWS = 256
NCH = 5
SUB = 48
NSUB = TOK // SUB
HALF = TOK // 2
STEPS = 4
WIN = STEPS * TOK + HD
NEG = -1e30
EXP_SCALE = HD ** (-0.5) * 1.4426950408889634


class Plan:
    def __init__(self):
        self.tasks = []
        self.waits = {}

    def token(self, name, wait=None):
        self.waits[name] = wait
        return name

    def add(self, name, deps, dur, prio, emit, sends=()):
        self.tasks.append((name, list(deps), dur, prio, emit, list(sends)))

    def order(self, start):
        ready = {name: 0.0 for name in start}
        free = {}
        now = 0.0
        left = list(self.tasks)
        done = []
        while left:
            best = None
            soonest = None
            for task in left:
                if all(d in ready for d in task[1]):
                    at = max([ready[d] for d in task[1]], default=0.0)
                    if at <= now:
                        if best is None or task[3] < best[3]:
                            best = task
                    elif soonest is None or at < soonest:
                        soonest = at
            if best is None:
                now = soonest
                continue
            left.remove(best)
            done.append(best)
            now += best[2]
            ready["done:" + best[0]] = now
            for link, dur, lat, token in best[5]:
                begin = max(now, free.get(link, 0.0))
                free[link] = begin + dur
                ready[token] = begin + dur + lat
        self.total = now
        return done

    def emit(self, start):
        waited = set()
        for name, deps, _, _, emit, _ in self.order(start):
            for d in deps:
                if d not in waited and self.waits.get(d) is not None:
                    self.waits[d]()
                waited.add(d)
            emit()


def body(
    x_hbm, g_ref, w_hbm, mask_ref, cos_hbm, sin_hbm, o_hbm,
    xv, wv, cosv, sinv, hid, nrm, wts, part, got, acc, qbuf, kvb, out, sq, tot, rs,
    in_s, wz_s, wz_r, ws_s, ws_r, hx_s, hx_r, hy_s, hy_r, sq_s, sq_r, tx_s, tx_r,
    pr_s, pr_r, kv_s, kv_r, o_s,
):
    ci = lax.axis_index("ctx")
    fi = lax.axis_index("fsdp")
    xh, z, c = ci // 16, (ci // 2) % 8, ci % 2
    xl, y = fi // 4, fi % 4
    inner = xh != xl

    def dev(xh_, z_, c_, xl_, y_):
        return (xh_ * 16 + z_ * 2 + c_, xl_ * 4 + y_)

    up = dev(xh, (z + 1) % 8, c, xl, y)
    down = dev(xh, (z + 7) % 8, c, xl, y)
    sib = dev(xh, z, 1 - c, xl, y)
    far = dev(1 - xh, z, c, xl, y)
    cross = dev(1 - xh, z, c, 1 - xl, y)
    side = dev(xh, z, c, 1 - xl, y)
    yup = dev(xh, z, c, xl, (y + 1) % 4)
    ydown = dev(xh, z, c, xl, (y + 3) % 4)
    after = ((ci + 2) % 32, fi)
    before = ((ci + 30) % 32, fi)
    peers = [(ci, (fi + k) % 8) for k in range(1, 8)]

    started = []

    def remote(src, dst, s, r, to):
        return pltpu.make_async_remote_copy(
            src_ref=src, dst_ref=dst, send_sem=s, recv_sem=r, device_id=to, device_id_type=MESH
        )

    def send(*args):
        cp = remote(*args)
        cp.start()
        started.append(cp)

    load_w = pltpu.make_async_copy(w_hbm, wv, in_s.at[0])
    load_x = pltpu.make_async_copy(x_hbm, xv, in_s.at[1])
    load_c = pltpu.make_async_copy(cos_hbm, cosv, in_s.at[2])
    load_n = pltpu.make_async_copy(sin_hbm, sinv, in_s.at[3])
    load_h = pltpu.make_async_copy(x_hbm, hid.at[1, y], in_s.at[4])
    load_w.start()
    load_x.start()
    load_c.start()
    load_n.start()

    @pl.when(jnp.logical_not(inner))
    def _():
        load_h.start()

    barrier = pltpu.get_barrier_semaphore()
    greeted = peers + [far, cross, up, down, sib, after, before]
    for d in greeted:
        pl.semaphore_signal(barrier, inc=1, device_id=d, device_id_type=MESH)

    load_w.wait()
    own_piece = z * 2 + c

    def piece(j, idx):
        return wts.at[j, pl.ds(pl.multiple_of(idx * ROWS, ROWS), ROWS)]

    for j in range(NCH):
        for half in range(2):
            head = 8 + half if j == 0 else 2 * (j - 1) + half
            for rb in range(2):
                keep = mask_ref[rb, head].astype(F32)
                block = wv[rb * 128:(rb + 1) * 128, head * 128:(head + 1) * 128].astype(F32)
                wts[j, pl.ds(pl.multiple_of(own_piece * ROWS + rb * 128, 128), 128), half * 128:(half + 1) * 128] = (
                    block * keep
                ).astype(BF16)
    load_x.wait()

    lanes = jnp.zeros((TOK, 128), F32)
    for k in range(WID // 128):
        v = xv[:, k * 128:(k + 1) * 128].astype(F32)
        lanes = lanes + v * v
    sums = lax.dot_general(
        jnp.ones((8, 128), F32), lanes, (((1,), (1,)), ((), ())),
        precision=lax.Precision.HIGHEST, preferred_element_type=F32,
    )
    sq[fi] = sums
    pl.semaphore_wait(barrier, len(greeted))
    for k in range(1, 8):
        send(sq.at[fi], sq.at[fi], sq_s.at[k - 1], sq_r.at[k - 1], peers[k - 1])


    def hrows(m):
        return pl.ds(m * SUB, SUB)

    first_to = (
        jnp.where(inner, cross[0], side[0]),
        jnp.where(inner, cross[1], side[1]),
    )
    first_t = jnp.where(inner, 0, 1)

    def first_send(m):
        send(xv.at[hrows(m)], hid.at[first_t, y, hrows(m)], hx_s.at[0, m], hx_r.at[first_t, m], first_to)

    def own_send(j):
        src = piece(j, own_piece)
        send(src, src, wz_s.at[j, 0, 0], wz_r.at[j, 0, 0], up)
        send(src, src, wz_s.at[j, 1, 0], wz_r.at[j, 1, 0], down)
        send(src, src, ws_s.at[j, 0], ws_r.at[j, 0], sib)

    first_send(0)
    own_send(0)
    first_send(1)
    own_send(1)
    first_send(2)

    @pl.when(jnp.logical_not(inner))
    def _():
        load_h.wait()

    plan = Plan()
    start = []

    def at(step):
        return ((z + 8 + step) % 8) * 2 + c

    pz, lz = 2.9, 1.5

    def wait_w(j, way, d):
        def go():
            if d < 3:
                ref = piece(j, at(-(d + 1) if way == 0 else d + 1))
            else:
                ref = wts.at[j, pl.ds(pl.multiple_of(at(4) * ROWS + way * 128, 128), 128)]
            remote(ref, ref, wz_s.at[j, way, d], wz_r.at[j, way, d], sib).wait_recv()
        return go

    def wait_s(j, k):
        def go():
            ref = wts.at[j, pl.ds(0, ROWS)]
            remote(ref, ref, ws_s.at[j, k], ws_r.at[j, k], sib).wait_recv()
        return go

    for j in range(NCH):
        for way in range(2):
            for d in range(4):
                plan.token(f"w{j}{way}{d}", wait_w(j, way, d))
        for k in range(8):
            plan.token(f"s{j}{k}", wait_s(j, k))

    def own_task(j):
        plan.add(
            f"own{j}", [f"done:w{j-2}02f", f"done:w{j-2}12f"] if j >= 2 else [], 0.3, 0,
            (lambda: own_send(j)) if j >= 2 else (lambda: None),
            [("zu", pz, lz, f"w{j}00"), ("zd", pz, lz, f"w{j}10"), ("cc", 0.6, 1.0, f"s{j}0")],
        )

    def fwd_task(j, way, d):
        def go():
            idx = at(-(d + 1) if way == 0 else d + 1)
            to = up if way == 0 else down
            if d < 2:
                src = piece(j, idx)
            else:
                src = wts.at[j, pl.ds(pl.multiple_of(idx * ROWS + way * 128, 128), 128)]
            send(src, src, wz_s.at[j, way, d + 1], wz_r.at[j, way, d + 1], to)
            src = piece(j, idx)
            k = 1 + way * 3 + d
            send(src, src, ws_s.at[j, k], ws_r.at[j, k], sib)
        link = "zu" if way == 0 else "zd"
        plan.add(
            f"w{j}{way}{d}f", [f"w{j}{way}{d}"], 0.2, 1, go,
            [(link, pz if d < 2 else pz / 2, lz, f"w{j}{way}{d+1}"), ("cc", 0.6, 1.0, f"s{j}{1+way*3+d}")],
        )

    def last_task(j):
        def go():
            src = piece(j, at(4))
            send(src, src, ws_s.at[j, 7], ws_r.at[j, 7], sib)
        plan.add(f"w{j}l", [f"w{j}03", f"w{j}13"], 0.1, 1, go, [("cc", 0.6, 1.0, f"s{j}7")])

    for j in range(NCH):
        own_task(j)
        for way in range(2):
            for d in range(3):
                fwd_task(j, way, d)
        last_task(j)
    chunk_in = [
        [f"s{j}{k}" for k in range(8)]
        + [f"done:w{j}{way}{d}f" for way in range(2) for d in range(3)]
        + [f"done:w{j}l"]
        for j in range(NCH)
    ]

    ph, lh = 2.2, 1.5

    def hpiece(t, yy, m):
        return hid.at[t, yy, hrows(m)]

    def wait_hx(t, m):
        ref = hpiece(t, y, m)
        remote(ref, ref, hx_s.at[0, m], hx_r.at[t, m], sib).wait_recv()

    def y_sends(t, m):
        ref = hpiece(t, y, m)
        send_when.append(remote(ref, ref, hy_s.at[t, m, 0], hy_r.at[t, m, 0], yup))
        send_when[-1].start()
        send_when.append(remote(ref, ref, hy_s.at[t, m, 1], hy_r.at[t, m, 1], ydown))
        send_when[-1].start()

    send_when = []
    y_links = lambda t, m: [("yu", ph, lh, f"y{t}{m}0"), ("yd", ph, lh, f"y{t}{m}1")]
    seq = [(1, 0), (0, 0), (1, 1), (0, 1)] + [(0, m) for m in range(2, NSUB)] + [(1, m) for m in range(2, NSUB)]
    rank = {tm: n for n, tm in enumerate(seq)}

    def more(m):
        if m + 3 < NSUB:
            src = xv.at[hrows(m + 3)]
            remote(src, hid.at[first_t, y, hrows(m + 3)], hx_s.at[0, m + 3], hx_r.at[first_t, m + 3], first_to).start()

    def x_in(m):
        def go():
            @pl.when(inner)
            def _():
                wait_hx(0, m)
                ref = hpiece(0, y, m)
                remote(ref, ref, hx_s.at[1, m], hx_r.at[0, m], side).start()
                y_sends(0, m)
                more(m)
        plan.add(
            f"xi0{m}", [f"xa0{m}"], 0.1, 2, go,
            [("xo", ph, lh, f"xb0{m}")] + ([("xi", ph, lh, f"xa0{m+3}")] if m + 3 < NSUB else []),
        )

    def x_out(m):
        def go():
            @pl.when(jnp.logical_not(inner))
            def _():
                wait_hx(0, m)
                y_sends(0, m)
                more(m)
        plan.add(
            f"xo0{m}", [f"xb0{m}"], 0.1, 2, go,
            y_links(0, m) + ([("xs", ph, lh, f"xc1{m+3}")] if m + 3 < NSUB else []),
        )

    def x_own(m):
        def go():
            @pl.when(inner)
            def _():
                wait_hx(1, m)
            y_sends(1, m)
        deps = [f"xc1{m}"] + ([f"done:xo0{NSUB-1}"] if m >= 2 else [])
        plan.add(f"xo1{m}", deps, 0.1, 3, go, y_links(1, m))

    plan.add(
        "first", [], 0.5, -1, lambda: None,
        [("xi", ph, lh, f"xa0{m}") for m in range(3)] + [("xs", ph, lh, f"xc1{m}") for m in range(3)],
    )
    for m in range(NSUB):
        x_in(m)
        x_out(m)
        x_own(m)

    def wait_y(t, m, k):
        def go():
            idx = (y + 3) % 4 if k == 0 else (y + 1) % 4 if k == 1 else (y + 2) % 4
            ref = hpiece(t, idx, m)
            remote(ref, ref, hy_s.at[t, m, k], hy_r.at[t, m, k], sib).wait_recv()
        return go

    def y_task(t, m):
        way = m % 2
        for k in range(3):
            plan.token(f"y{t}{m}{k}", wait_y(t, m, k))

        def go():
            ref = hpiece(t, (y + 3) % 4 if way == 0 else (y + 1) % 4, m)
            send(ref, ref, hy_s.at[t, m, 2], hy_r.at[t, m, 2], yup if way == 0 else ydown)
        plan.add(
            f"yf{t}{m}", [f"y{t}{m}{way}"], 0.1, 2, go, [("yu" if way == 0 else "yd", ph, lh, f"y{t}{m}2")]
        )

    def wait_sq(k):
        def go():
            remote(sq.at[0], sq.at[0], sq_s.at[k], sq_r.at[k], sib).wait_recv()
        return go

    def spread(which, rows8):
        inv = lax.rsqrt(rows8 * (1.0 / 8192.0) + 1e-05)
        rs[which] = lax.dot_general(
            inv, jnp.full((8, 128), 0.125, F32), (((0,), (0,)), ((), ())),
            precision=lax.Precision.HIGHEST, preferred_element_type=F32,
        )

    def total():
        rows8 = sq[0]
        for k in range(1, 8):
            rows8 = rows8 + sq[k]
        tot[1] = rows8
        send(tot.at[1], tot.at[0], tx_s.at[0], tx_r.at[0], far)
        spread(1, rows8)

    def wait_tx():
        remote(tot.at[1], tot.at[0], tx_s.at[0], tx_r.at[0], far).wait_recv()

    plan.token("tx", wait_tx)
    for k in range(7):
        start.append(plan.token(f"sq{k}", wait_sq(k)))
    plan.add("sqa", ["done:first"], 3.0, 0, lambda: None)
    plan.add("total", [f"sq{k}" for k in range(7)] + ["done:sqa"], 0.5, 1, total, [("none", 0, 2.5, "tx")])
    plan.add("other", ["tx"], 0.5, 1, lambda: spread(0, tot[0]))

    def norm_task(t, m, step, deps):
        def go():
            yy = (y + step) % 4
            gain = g_ref[pl.ds(xh * 4 + yy, 1), :]
            scale = rs[t, m * SUB:(m + 1) * SUB, :]
            for k in range(WID // 128):
                v = hid[t, yy, m * SUB:(m + 1) * SUB, k * 128:(k + 1) * 128].astype(F32)
                v = v * scale * gain[:, k * 128:(k + 1) * 128]
                nrm[t, m * SUB:(m + 1) * SUB, pl.ds(pl.multiple_of(yy * WID + k * 128, 128), 128)] = v.astype(BF16)
        plan.add(f"n{t}{m}{step}", deps + ["done:other" if t == 0 else "done:total"], 0.15, 4 + rank[(t, m)] * 0.01, go)

    for t in range(2):
        for m in range(NSUB):
            y_task(t, m)
            norm_task(t, m, 0, [f"done:xo{t}{m}"] + ([f"done:xi{t}{m}"] if t == 0 else []))
            norm_task(t, m, 3, [f"y{t}{m}0"])
            norm_task(t, m, 1, [f"y{t}{m}1"])
            norm_task(t, m, 2, [f"y{t}{m}2"])

    per_half = NSUB // 2

    def normed_in(t, h):
        return [f"done:n{t}{m}{s}" for m in range(h * per_half, (h + 1) * per_half) for s in range(4)]

    def product(t, h, j):
        return jnp.dot(nrm[t, h * HALF:(h + 1) * HALF, :], wts[j], preferred_element_type=F32)

    def wait_pr(j, h):
        def go():
            ref = got.at[j, pl.ds(h * HALF, HALF)]
            remote(ref, ref, pr_s.at[j, h], pr_r.at[j, h], far).wait_recv()
        return go

    def other_task(h, j):
        def go():
            rows = pl.ds(h * HALF, HALF)
            part[j, rows] = product(0, h, j)
            send(part.at[j, rows], got.at[j, rows], pr_s.at[j, h], pr_r.at[j, h], far)
        plan.token(f"p{j}{h}", wait_pr(j, h))
        plan.add(f"m0{h}{j}", normed_in(0, h) + chunk_in[j], 0.6, 5 + j * 0.1 + h * 0.01, go, [("xp", 4.4, 2.0, f"p{j}{h}")])

    def rotated(u, rows):
        return u * cosv[rows, :] + pltpu.roll(u, 64, 1) * sinv[rows, :]

    def own_product(h, j):
        def go():
            rows = pl.ds(h * HALF, HALF)
            acc[j, rows] = product(1, h, j)
        plan.add(f"m1{h}{j}", normed_in(1, h) + chunk_in[j], 0.6, 6 + j * 0.1 + h * 0.01, go)

    def kv_send(blk_from, blk_to, h, k, to):
        rows = pl.ds(h * HALF, HALF)
        send(kvb.at[blk_from, rows], kvb.at[blk_to, rows], kv_s.at[k, h], kv_r.at[k, h], to)

    def finish(h, j):
        def go():
            rows = pl.ds(h * HALF, HALF)
            u = acc[j, rows] + got[j, rows]
            left, right = u[:, :HD], u[:, HD:]
            if j == 0:
                kvb[4 + c, rows, 0:HD] = rotated(left, rows).astype(BF16)
                kvb[4 + c, rows, HD:2 * HD] = right.astype(BF16)
                kv_send(4 + c, 2 + c, h, 0, after)
                kv_send(4 + c, 4 + c, h, 2, sib)
            else:
                qbuf[j - 1, rows, 0:HD] = rotated(left, rows).astype(BF16)
                qbuf[j - 1, rows, HD:2 * HD] = rotated(right, rows).astype(BF16)
        sends = [("zu", 2.2, 2.0, f"k0{h}"), ("cc", 0.3, 1.0, f"k2{h}")] if j == 0 else []
        plan.add(f"f{h}{j}", [f"done:m1{h}{j}", f"p{j}{h}", "done:rope"], 0.3, 4.5 + j * 0.1, go, sends)

    def rope():
        load_c.wait()
        load_n.wait()

    plan.add("rope", [], 0.1, 20, rope)

    def wait_kv(k, h):
        def go():
            ref = kvb.at[0, pl.ds(0, HALF)]
            remote(ref, ref, kv_s.at[k, h], kv_r.at[k, h], sib).wait_recv()
        return go

    for h in range(2):
        for k in range(5):
            plan.token(f"k{k}{h}", wait_kv(k, h))

        def pass_one(h=h):
            kv_send(2 + c, c, h, 1, after)
            kv_send(2 + c, 2 + c, h, 3, sib)

        def pass_two(h=h):
            kv_send(c, c, h, 4, sib)

        plan.add(f"ka{h}", [f"k0{h}"], 0.1, 1, pass_one, [("zu", 2.2, 2.0, f"k1{h}"), ("cc", 0.3, 1.0, f"k3{h}")])
        plan.add(f"kb{h}", [f"k1{h}"], 0.1, 1, pass_two, [("cc", 0.3, 1.0, f"k4{h}")])
        for j in range(NCH):
            other_task(h, j)
            own_product(h, j)
            finish(h, j)
    window_in = [f"k{k}{h}" for k in (2, 3, 4) for h in range(2)] + [f"done:kb{h}" for h in range(2)] + [f"done:f{h}0" for h in range(2)]

    def attend(j):
        def go():
            row = lax.broadcasted_iota(jnp.int32, (HD, HD), 0)
            col = lax.broadcasted_iota(jnp.int32, (HD, HD), 1)
            later = col > row
            key_at = lax.broadcasted_iota(jnp.int32, (1, WIN), 1)

            def block(b, carry):
                r0 = pl.multiple_of(b * HD, HD)
                k0 = pl.multiple_of(c * TOK + b * HD, HD)
                keys = kvf[pl.ds(k0, WIN), 0:HD]
                vals = kvf[pl.ds(k0, WIN), HD:2 * HD]
                real = key_at >= (STEPS - ci) * TOK - b * HD
                for half in range(2):
                    q = qbuf[j - 1, pl.ds(r0, HD), half * HD:(half + 1) * HD]
                    s = lax.dot_general(q, keys, (((1,), (1,)), ((), ())), preferred_element_type=F32)
                    s = jnp.concatenate(
                        [
                            jnp.where(later, s[:, :HD], NEG),
                            s[:, HD:WIN - HD],
                            jnp.where(later, NEG, s[:, WIN - HD:]),
                        ],
                        axis=1,
                    )
                    s = jnp.where(real, s, NEG)
                    peak = jnp.max(s, axis=1, keepdims=True)
                    e = jnp.exp2((s - peak) * EXP_SCALE)
                    probs = (e * (1.0 / jnp.sum(e, axis=1, keepdims=True))).astype(BF16)
                    o = jnp.dot(probs, vals, preferred_element_type=F32)
                    out[j - 1, pl.ds(r0, HD), half * HD:(half + 1) * HD] = o.astype(BF16)
                return carry

            lax.fori_loop(0, TOK // HD, block, 0)
            pltpu.make_async_copy(out.at[j - 1], o_hbm.at[:, pl.ds((j - 1) * 256, 256)], o_s.at[j - 1]).start()
        plan.add(f"a{j}", window_in + [f"done:f{h}{j}" for h in range(2)], 3.0, 7 + j, go)

    kvf = kvb.reshape(6 * TOK, 2 * HD)
    for j in range(1, NCH):
        attend(j)

    plan.emit(start)
    body.total = plan.total

    for j in range(1, NCH):
        pltpu.make_async_copy(out.at[j - 1], o_hbm.at[:, pl.ds((j - 1) * 256, 256)], o_s.at[j - 1]).wait()
    for cp in started:
        cp.wait_send()
    for t in range(2):
        for m in range(NSUB):
            for k in range(2):
                ref = hpiece(t, y, m)
                remote(ref, ref, hy_s.at[t, m, k], hy_r.at[t, m, k], yup).wait_send()

    for m in range(3, NSUB):
        remote(xv.at[hrows(m)], hid.at[first_t, y, hrows(m)], hx_s.at[0, m], hx_r.at[first_t, m], first_to).wait_send()

    @pl.when(inner)
    def _():
        for m in range(NSUB):
            ref = hpiece(0, y, m)
            remote(ref, ref, hx_s.at[1, m], hx_r.at[0, m], side).wait_send()


def shards(hidden_states, norm_gain, qkv_weight, block_mask):
    ci = lax.axis_index("ctx")
    position = (ci * TOK + jnp.arange(TOK, dtype=jnp.int32)).astype(F32)
    inverse = jnp.power(F32(500000.0), -(jnp.arange(0, HD, 2).astype(F32) / HD))
    angles = position[:, None] * inverse[None, :]
    cosine, sine = jnp.cos(angles), jnp.sin(angles)
    cos2 = jnp.concatenate([cosine, cosine], axis=1)
    sin2 = jnp.concatenate([-sine, sine], axis=1)
    gain = norm_gain.astype(F32).reshape(8, WID)
    any_ = pl.BlockSpec(memory_space=pl.ANY)
    dma = pltpu.SemaphoreType.DMA
    result = pl.pallas_call(
        body,
        out_shape=jax.ShapeDtypeStruct((TOK, 1024), BF16),
        in_specs=[
            any_, pl.BlockSpec(memory_space=pltpu.VMEM), any_, pl.BlockSpec(memory_space=pltpu.SMEM), any_, any_,
        ],
        out_specs=any_,
        scratch_shapes=[
            pltpu.VMEM((TOK, WID), BF16),
            pltpu.VMEM((ROWS, 1280), BF16),
            pltpu.VMEM((TOK, HD), F32),
            pltpu.VMEM((TOK, HD), F32),
            pltpu.VMEM((2, 4, TOK, WID), BF16),
            pltpu.VMEM((2, TOK, KH), BF16),
            pltpu.VMEM((NCH, KH, 256), BF16),
            pltpu.VMEM((NCH, TOK, 256), F32),
            pltpu.VMEM((NCH, TOK, 256), F32),
            pltpu.VMEM((NCH, TOK, 256), F32),
            pltpu.VMEM((4, TOK, 256), BF16),
            pltpu.VMEM((6, TOK, 256), BF16),
            pltpu.VMEM((4, TOK, 256), BF16),
            pltpu.VMEM((8, 8, TOK), F32),
            pltpu.VMEM((2, 8, TOK), F32),
            pltpu.VMEM((2, TOK, HD), F32),
            dma((5,)),
            dma((NCH, 2, 4)), dma((NCH, 2, 4)),
            dma((NCH, 8)), dma((NCH, 8)),
            dma((2, NSUB)), dma((2, NSUB)),
            dma((2, NSUB, 3)), dma((2, NSUB, 3)),
            dma((7,)), dma((7,)),
            dma((1,)), dma((1,)),
            dma((NCH, 2)), dma((NCH, 2)),
            dma((5, 2)), dma((5, 2)),
            dma((4,)),
        ],
        compiler_params=pltpu.CompilerParams(
            collective_id=0, has_side_effects=True, vmem_limit_bytes=58 * 2**20
        ),
        cost_estimate=pl.CostEstimate(flops=12 * 10**9, bytes_accessed=3 * 10**6, transcendentals=6 * 10**6),
    )(
        hidden_states, gain, qkv_weight.reshape(ROWS, 1280), block_mask.reshape(2, 10), cos2, sin2,
    )
    return result.reshape(TOK, 1, 1024)


def solution(mesh):
    return jax.shard_map(
        shards,
        mesh=mesh,
        in_specs=(P("ctx", "fsdp"), P(), P("ctx", "fsdp", None), P("ctx", "fsdp", None)),
        out_specs=P("ctx", "fsdp", None),
        check_vma=False,
    )
```

```python
import jax
import jax.numpy as jnp
from jax import lax
from jax.experimental import pallas as pl
from jax.experimental.pallas import tpu as pltpu
from jax.sharding import PartitionSpec as P

MESH = pl.DeviceIdType.MESH
F32 = jnp.float32
BF16 = jnp.bfloat16
HD = 128
TOK = 384
WID = 1024
KH = 4096
ROWS = 256
NCH = 5
SUB = 48
NSUB = TOK // SUB
HALF = TOK // 2
STEPS = 4
WIN = STEPS * TOK + HD
NEG = -1e30
BACK = (2, 2, 2)
EARLY = 0
OWN = 1
AHEAD = 3
TGROUPS = (((0, 2), (2, 4), (4, 6), (6, 8)), ((0, 4), (4, 8)))
QGROUPS = ((0, 4), (4, 8))
KGROUPS = ((0, 4), (4, 6), (6, 8))
EXP_SCALE = HD ** (-0.5) * 1.4426950408889634


class Plan:
    def __init__(self):
        self.tasks = []
        self.waits = {}

    def token(self, name, wait=None):
        self.waits[name] = wait
        return name

    def add(self, name, deps, dur, prio, emit, sends=()):
        self.tasks.append((name, list(deps), dur, prio, emit, list(sends)))

    def order(self, start):
        ready = {name: 0.0 for name in start}
        free = {}
        now = 0.0
        left = list(self.tasks)
        done = []
        while left:
            best = None
            soonest = None
            for task in left:
                if all(d in ready for d in task[1]):
                    at = max([ready[d] for d in task[1]], default=0.0)
                    if at <= now:
                        if best is None or task[3] < best[3]:
                            best = task
                    elif soonest is None or at < soonest:
                        soonest = at
            if best is None:
                now = soonest
                continue
            left.remove(best)
            done.append(best)
            now += best[2]
            ready["done:" + best[0]] = now
            for link, dur, lat, token in best[5]:
                begin = max(now, free.get(link, 0.0))
                free[link] = begin + dur
                ready[token] = begin + dur + lat
        self.total = now
        return done

    def emit(self, start):
        waited = set()
        for name, deps, _, _, emit, _ in self.order(start):
            for d in deps:
                if d not in waited and self.waits.get(d) is not None:
                    self.waits[d]()
                waited.add(d)
            emit()


def body(
    x_hbm, g_ref, w_hbm, mask_ref, cos_hbm, sin_hbm, o_ref,
    xv, wv, half_c, half_n, cosv, sinv, hid, nrm, wts, part, got, acc, qbuf, kvb, sq, tot, rs,
    in_s, wz_s, wz_r, ws_s, ws_r, hx_s, hx_r, hy_s, hy_r, sq_s, sq_r, tx_s, tx_r,
    pr_s, pr_r, kv_s, kv_r,
):
    ci = lax.axis_index("ctx")
    fi = lax.axis_index("fsdp")
    xh, z, c = ci // 16, (ci // 2) % 8, ci % 2
    xl, y = fi // 4, fi % 4
    inner = xh != xl

    def dev(xh_, z_, c_, xl_, y_):
        return (xh_ * 16 + z_ * 2 + c_, xl_ * 4 + y_)

    up = dev(xh, (z + 1) % 8, c, xl, y)
    down = dev(xh, (z + 7) % 8, c, xl, y)
    sib = dev(xh, z, 1 - c, xl, y)
    far = dev(1 - xh, z, c, xl, y)
    cross = dev(1 - xh, z, c, 1 - xl, y)
    side = dev(xh, z, c, 1 - xl, y)
    yup = dev(xh, z, c, xl, (y + 1) % 4)
    ydown = dev(xh, z, c, xl, (y + 3) % 4)
    after = ((ci + 2) % 32, fi)
    before = ((ci + 30) % 32, fi)
    peers = [(ci, (fi + k) % 8) for k in range(1, 8)]

    started = []

    def remote(src, dst, s, r, to):
        return pltpu.make_async_remote_copy(
            src_ref=src, dst_ref=dst, send_sem=s, recv_sem=r, device_id=to, device_id_type=MESH
        )

    def send(*args):
        cp = remote(*args)
        cp.start()
        started.append(cp)

    load_w = pltpu.make_async_copy(w_hbm, wv, in_s.at[0])
    load_x = pltpu.make_async_copy(x_hbm, xv, in_s.at[1])
    load_c = pltpu.make_async_copy(cos_hbm, half_c, in_s.at[2])
    load_n = pltpu.make_async_copy(sin_hbm, half_n, in_s.at[3])
    load_h = pltpu.make_async_copy(x_hbm, hid.at[1, y], in_s.at[4])
    load_w.start()
    load_x.start()
    load_c.start()
    load_n.start()

    @pl.when(jnp.logical_not(inner))
    def _():
        load_h.start()

    barrier = pltpu.get_barrier_semaphore()
    greeted = peers + [far, cross, up, down, sib, after, before]
    for d in greeted:
        pl.semaphore_signal(barrier, inc=1, device_id=d, device_id_type=MESH)

    load_w.wait()
    own_piece = z * 2 + c

    def piece(j, idx):
        return wts.at[j, pl.ds(pl.multiple_of(idx * ROWS, ROWS), ROWS)]

    for j in range(NCH):
        for half in range(2):
            head = 8 + half if j == 0 else 2 * (j - 1) + half
            for rb in range(2):
                keep = mask_ref[rb, head].astype(F32)
                block = wv[rb * 128:(rb + 1) * 128, head * 128:(head + 1) * 128].astype(F32)
                wts[j, pl.ds(pl.multiple_of(own_piece * ROWS + rb * 128, 128), 128), half * 128:(half + 1) * 128] = (
                    block * keep
                ).astype(BF16)
    load_x.wait()

    lanes = jnp.zeros((TOK, 128), F32)
    for k in range(WID // 128):
        v = xv[:, k * 128:(k + 1) * 128].astype(F32)
        lanes = lanes + v * v
    sums = lax.dot_general(
        jnp.ones((8, 128), F32), lanes, (((1,), (1,)), ((), ())),
        precision=lax.Precision.HIGHEST, preferred_element_type=F32,
    )
    sq[fi] = sums
    pl.semaphore_wait(barrier, len(greeted))
    for k in range(1, 8):
        send(sq.at[fi], sq.at[fi], sq_s.at[k - 1], sq_r.at[k - 1], peers[k - 1])


    def hrows(m):
        return pl.ds(m * SUB, SUB)

    first_to = (
        jnp.where(inner, cross[0], side[0]),
        jnp.where(inner, cross[1], side[1]),
    )
    first_t = jnp.where(inner, 0, 1)

    def first_send(m):
        send(xv.at[hrows(m)], hid.at[first_t, y, hrows(m)], hx_s.at[0, m], hx_r.at[first_t, m], first_to)

    def own_send(j):
        src = piece(j, own_piece)
        send(src, src, wz_s.at[j, 0, 0], wz_r.at[j, 0, 0], up)
        send(src, src, wz_s.at[j, 1, 0], wz_r.at[j, 1, 0], down)
        send(src, src, ws_s.at[j, 0], ws_r.at[j, 0], sib)

    first_send(0)
    own_send(0)
    first_send(1)
    for j in range(1, BACK[2]):
        own_send(j)
    first_send(2)

    @pl.when(jnp.logical_not(inner))
    def _():
        load_h.wait()

    plan = Plan()
    start = []

    def at(step):
        return ((z + 8 + step) % 8) * 2 + c

    pz, lz = 2.9, 1.5

    def wait_w(j, way, d):
        def go():
            if d < 3:
                ref = piece(j, at(-(d + 1) if way == 0 else d + 1))
            else:
                ref = wts.at[j, pl.ds(pl.multiple_of(at(4) * ROWS + way * 128, 128), 128)]
            remote(ref, ref, wz_s.at[j, way, d], wz_r.at[j, way, d], sib).wait_recv()
        return go

    def wait_s(j, k):
        def go():
            ref = wts.at[j, pl.ds(0, ROWS)]
            remote(ref, ref, ws_s.at[j, k], ws_r.at[j, k], sib).wait_recv()
        return go

    for j in range(NCH):
        for way in range(2):
            for d in range(4):
                plan.token(f"w{j}{way}{d}", wait_w(j, way, d))
        for k in range(8):
            plan.token(f"s{j}{k}", wait_s(j, k))

    def own_task(j):
        plan.add(
            f"own{j}", [f"done:w{j-BACK[0]}{way}{BACK[1]}f" for way in range(2)] if j >= BACK[2] else [], 0.3, 0,
            (lambda: own_send(j)) if j >= BACK[2] else (lambda: None),
            [("zu", pz, lz, f"w{j}00"), ("zd", pz, lz, f"w{j}10"), ("cc", 0.6, 1.0, f"s{j}0")],
        )

    def fwd_task(j, way, d):
        def go():
            idx = at(-(d + 1) if way == 0 else d + 1)
            to = up if way == 0 else down
            if d < 2:
                src = piece(j, idx)
            else:
                src = wts.at[j, pl.ds(pl.multiple_of(idx * ROWS + way * 128, 128), 128)]
            send(src, src, wz_s.at[j, way, d + 1], wz_r.at[j, way, d + 1], to)
            src = piece(j, idx)
            k = 1 + way * 3 + d
            send(src, src, ws_s.at[j, k], ws_r.at[j, k], sib)
        link = "zu" if way == 0 else "zd"
        plan.add(
            f"w{j}{way}{d}f", [f"w{j}{way}{d}"], 0.2, 1, go,
            [(link, pz if d < 2 else pz / 2, lz, f"w{j}{way}{d+1}"), ("cc", 0.6, 1.0, f"s{j}{1+way*3+d}")],
        )

    def last_task(j):
        def go():
            src = piece(j, at(4))
            send(src, src, ws_s.at[j, 7], ws_r.at[j, 7], sib)
        plan.add(f"w{j}l", [f"w{j}03", f"w{j}13"], 0.1, 1, go, [("cc", 0.6, 1.0, f"s{j}7")])

    for j in range(NCH):
        own_task(j)
        for way in range(2):
            for d in range(3):
                fwd_task(j, way, d)
        last_task(j)
    chunk_in = [
        [f"s{j}{k}" for k in range(8)]
        + [f"done:w{j}{way}{d}f" for way in range(2) for d in range(3)]
        + [f"done:w{j}l"]
        for j in range(NCH)
    ]

    ph, lh = 2.2, 1.5

    def hpiece(t, yy, m):
        return hid.at[t, yy, hrows(m)]

    def wait_hx(t, m):
        ref = hpiece(t, y, m)
        remote(ref, ref, hx_s.at[0, m], hx_r.at[t, m], sib).wait_recv()

    def y_sends(t, m):
        ref = hpiece(t, y, m)
        send_when.append(remote(ref, ref, hy_s.at[t, m, 0], hy_r.at[t, m, 0], yup))
        send_when[-1].start()
        send_when.append(remote(ref, ref, hy_s.at[t, m, 1], hy_r.at[t, m, 1], ydown))
        send_when[-1].start()

    send_when = []
    y_links = lambda t, m: [("yu", ph, lh, f"y{t}{m}0"), ("yd", ph, lh, f"y{t}{m}1")]
    seq = [(0, m) for m in range(EARLY)] + [(1, m) for m in range(OWN)] + [(0, m) for m in range(EARLY, NSUB)] + [(1, m) for m in range(OWN, NSUB)]
    rank = {tm: n for n, tm in enumerate(seq)}

    def more(m):
        if m + 3 < NSUB:
            src = xv.at[hrows(m + 3)]
            remote(src, hid.at[first_t, y, hrows(m + 3)], hx_s.at[0, m + 3], hx_r.at[first_t, m + 3], first_to).start()

    def x_in(m):
        def go():
            @pl.when(inner)
            def _():
                wait_hx(0, m)
                ref = hpiece(0, y, m)
                remote(ref, ref, hx_s.at[1, m], hx_r.at[0, m], side).start()
                more(m)
        plan.add(
            f"xi0{m}", [f"xa0{m}"], 0.1, 2, go,
            [("xo", ph, lh, f"xb0{m}")] + ([("xi", ph, lh, f"xa0{m+3}")] if m + 3 < NSUB else []),
        )

    def x_out(m):
        def go():
            @pl.when(jnp.logical_not(inner))
            def _():
                wait_hx(0, m)
                more(m)
        plan.add(
            f"xo0{m}", [f"xb0{m}"], 0.1, 2, go,
            [("xs", ph, lh, f"xc1{m+3}")] if m + 3 < NSUB else [],
        )

    def x_own(m):
        def go():
            @pl.when(inner)
            def _():
                wait_hx(1, m)
        plan.add(f"xo1{m}", [f"xc1{m}"], 0.1, 3, go)

    def y_own(t, m):
        n = rank[(t, m)]
        deps = [f"done:xo{t}{m}"] + ([f"done:xi{t}{m}"] if t == 0 else [])
        if n >= AHEAD:
            deps.append("done:yf%d%d" % seq[n - AHEAD])
        plan.add(f"ys{t}{m}", deps, 0.1, 1.5, lambda: y_sends(t, m), y_links(t, m))

    plan.add(
        "first", [], 0.5, -1, lambda: None,
        [("xi", ph, lh, f"xa0{m}") for m in range(3)] + [("xs", ph, lh, f"xc1{m}") for m in range(3)],
    )
    for m in range(NSUB):
        x_in(m)
        x_out(m)
        x_own(m)
        for t in range(2):
            y_own(t, m)

    def wait_y(t, m, k):
        def go():
            idx = (y + 3) % 4 if k == 0 else (y + 1) % 4 if k == 1 else (y + 2) % 4
            ref = hpiece(t, idx, m)
            remote(ref, ref, hy_s.at[t, m, k], hy_r.at[t, m, k], sib).wait_recv()
        return go

    def y_task(t, m):
        way = m % 2
        for k in range(3):
            plan.token(f"y{t}{m}{k}", wait_y(t, m, k))

        def go():
            ref = hpiece(t, (y + 3) % 4 if way == 0 else (y + 1) % 4, m)
            send(ref, ref, hy_s.at[t, m, 2], hy_r.at[t, m, 2], yup if way == 0 else ydown)
        plan.add(
            f"yf{t}{m}", [f"y{t}{m}{way}"], 0.1, 2, go, [("yu" if way == 0 else "yd", ph, lh, f"y{t}{m}2")]
        )

    def wait_sq(k):
        def go():
            remote(sq.at[0], sq.at[0], sq_s.at[k], sq_r.at[k], sib).wait_recv()
        return go

    def spread(which, rows8):
        inv = lax.rsqrt(rows8 * (1.0 / 8192.0) + 1e-05)
        rs[which] = lax.dot_general(
            inv, jnp.full((8, 128), 0.125, F32), (((0,), (0,)), ((), ())),
            precision=lax.Precision.HIGHEST, preferred_element_type=F32,
        )

    def total():
        rows8 = sq[0]
        for k in range(1, 8):
            rows8 = rows8 + sq[k]
        tot[1] = rows8
        send(tot.at[1], tot.at[0], tx_s.at[0], tx_r.at[0], far)
        spread(1, rows8)

    def wait_tx():
        remote(tot.at[1], tot.at[0], tx_s.at[0], tx_r.at[0], far).wait_recv()

    plan.token("tx", wait_tx)
    for k in range(7):
        start.append(plan.token(f"sq{k}", wait_sq(k)))
    plan.add("sqa", ["done:first"], 3.0, 0, lambda: None)
    plan.add("total", [f"sq{k}" for k in range(7)] + ["done:sqa"], 0.5, 1, total, [("none", 0, 2.5, "tx")])
    plan.add("other", ["tx"], 0.5, 1, lambda: spread(0, tot[0]))

    def norm_task(t, m, step, deps):
        def go():
            yy = (y + step) % 4
            gain = g_ref[pl.ds(xh * 4 + yy, 1), :]
            scale = rs[t, m * SUB:(m + 1) * SUB, :]
            for k in range(WID // 128):
                v = hid[t, yy, m * SUB:(m + 1) * SUB, k * 128:(k + 1) * 128].astype(F32)
                v = v * scale * gain[:, k * 128:(k + 1) * 128]
                nrm[t, m * SUB:(m + 1) * SUB, pl.ds(pl.multiple_of(yy * WID + k * 128, 128), 128)] = v.astype(BF16)
        plan.add(f"n{t}{m}{step}", deps + ["done:other" if t == 0 else "done:total"], 0.05, 4 + rank[(t, m)] * 0.01, go)

    for t in range(2):
        for m in range(NSUB):
            y_task(t, m)
            norm_task(t, m, 0, [f"done:xo{t}{m}"] + ([f"done:xi{t}{m}"] if t == 0 else []))
            norm_task(t, m, 3, [f"y{t}{m}0"])
            norm_task(t, m, 1, [f"y{t}{m}1"])
            norm_task(t, m, 2, [f"y{t}{m}2"])

    def product(t, lo, hi, j):
        return jnp.dot(nrm[t, lo * SUB:hi * SUB, :], wts[j], preferred_element_type=F32)

    def sent(j):
        return TGROUPS[0] if j < 2 else TGROUPS[1]

    def sent_rows(j, h):
        lo, hi = sent(j)[h]
        return pl.ds(lo * SUB, (hi - lo) * SUB)

    def wait_pr(j, h):
        def go():
            ref = got.at[j, sent_rows(j, h)]
            remote(ref, ref, pr_s.at[j, h], pr_r.at[j, h], far).wait_recv()
        return go

    def other_task(h, j):
        lo, hi = sent(j)[h]

        def go():
            rows = sent_rows(j, h)
            part[j, rows] = product(0, lo, hi, j)
            send(part.at[j, rows], got.at[j, rows], pr_s.at[j, h], pr_r.at[j, h], far)
        plan.token(f"p{j}{h}", wait_pr(j, h))
        deps = [f"done:n0{m}{s}" for m in range(lo, hi) for s in range(4)]
        plan.add(
            f"m0{h}{j}", deps + chunk_in[j], 1.0 if hi - lo > 2 else 0.7, 5 + j * 0.1 + h * 0.01, go,
            [("xp", 1.1 * (hi - lo), 2.0, f"p{j}{h}")],
        )

    def rotated(u, rows):
        return u * cosv[rows, :] + pltpu.roll(u, 64, 1) * sinv[rows, :]

    def groups(j):
        return KGROUPS if j == 0 else QGROUPS

    def own_product(h, j):
        lo, hi = groups(j)[h]

        def go():
            acc[j, pl.ds(lo * SUB, (hi - lo) * SUB)] = product(1, lo, hi, j)
        deps = [f"done:n1{m}{s}" for m in range(lo, hi) for s in range(4)]
        plan.add(f"m1{h}{j}", deps + chunk_in[j], 1.0 if hi - lo > 2 else 0.7, (4.4 if j == 0 else 6) + j * 0.1 + h * 0.01, go)

    def kv_send(blk_from, blk_to, h, k, to):
        lo, hi = KGROUPS[h]
        rows = pl.ds(lo * SUB, (hi - lo) * SUB)
        send(kvb.at[blk_from, rows], kvb.at[blk_to, rows], kv_s.at[k, h], kv_r.at[k, h], to)

    def kv_time(h):
        return 0.55 * (KGROUPS[h][1] - KGROUPS[h][0])

    def finish(h, j):
        lo, hi = groups(j)[h]

        def go():
            rows = pl.ds(lo * SUB, (hi - lo) * SUB)
            u = acc[j, rows] + got[j, rows]
            left, right = u[:, :HD], u[:, HD:]
            if j == 0:
                kvb[4 + c, rows, 0:HD] = rotated(left, rows).astype(BF16)
                kvb[4 + c, rows, HD:2 * HD] = right.astype(BF16)
                kv_send(4 + c, 2 + c, h, 0, after)
                kv_send(4 + c, 4 + c, h, 2, sib)
            else:
                qbuf[j - 1, rows, 0:HD] = rotated(left, rows).astype(BF16)
                qbuf[j - 1, rows, HD:2 * HD] = rotated(right, rows).astype(BF16)
        sends = [("zu", kv_time(h), 2.0, f"k0{h}"), ("cc", 0.3, 1.0, f"k2{h}")] if j == 0 else []
        parts = [p for p, (a, b) in enumerate(sent(j)) if a < hi and b > lo]
        plan.add(
            f"f{h}{j}", [f"done:m1{h}{j}", "done:rope"] + [f"p{j}{p}" for p in parts], 0.2, 4.5 + j * 0.1, go, sends
        )

    def rope():
        load_c.wait()
        load_n.wait()
        cosv[...] = jnp.concatenate([half_c[...], half_c[...]], axis=1)
        sinv[...] = jnp.concatenate([-half_n[...], half_n[...]], axis=1)

    plan.add("rope", ["done:other"], 0.5, 3.5, rope)

    def wait_kv(k, h):
        def go():
            ref = kvb.at[0, pl.ds(0, (KGROUPS[h][1] - KGROUPS[h][0]) * SUB)]
            remote(ref, ref, kv_s.at[k, h], kv_r.at[k, h], sib).wait_recv()
        return go

    for h in range(len(KGROUPS)):
        for k in range(5):
            plan.token(f"k{k}{h}", wait_kv(k, h))

        def pass_one(h=h):
            kv_send(2 + c, c, h, 1, after)
            kv_send(2 + c, 2 + c, h, 3, sib)

        def pass_two(h=h):
            kv_send(c, c, h, 4, sib)

        plan.add(f"ka{h}", [f"k0{h}"], 0.1, 1, pass_one, [("zu", kv_time(h), 2.0, f"k1{h}"), ("cc", 0.3, 1.0, f"k3{h}")])
        plan.add(f"kb{h}", [f"k1{h}"], 0.1, 1, pass_two, [("cc", 0.3, 1.0, f"k4{h}")])
    for j in range(NCH):
        for h in range(len(sent(j))):
            other_task(h, j)
        for h in range(len(groups(j))):
            own_product(h, j)
            finish(h, j)
    ngk = len(KGROUPS)
    window_in = [f"k{k}{h}" for k in (2, 3, 4) for h in range(ngk)] + [f"done:kb{h}" for h in range(ngk)] + [f"done:f{h}0" for h in range(ngk)]

    def attend(j):
        def go():
            row = lax.broadcasted_iota(jnp.int32, (2 * HD, HD), 0)
            col = lax.broadcasted_iota(jnp.int32, (2 * HD, HD), 1)
            later = col > row % HD
            key_at = lax.broadcasted_iota(jnp.int32, (1, WIN), 1)

            def block(b, carry):
                r0 = pl.multiple_of(b * HD, HD)
                k0 = pl.multiple_of(c * TOK + b * HD, HD)
                keys = kvf[pl.ds(k0, WIN), 0:HD]
                vals = kvf[pl.ds(k0, WIN), HD:2 * HD]
                real = key_at >= (STEPS - ci) * TOK - b * HD
                q = jnp.concatenate(
                    [qbuf[j - 1, pl.ds(r0, HD), 0:HD], qbuf[j - 1, pl.ds(r0, HD), HD:2 * HD]], axis=0
                )
                s = lax.dot_general(q, keys, (((1,), (1,)), ((), ())), preferred_element_type=F32)
                s = jnp.concatenate(
                    [
                        jnp.where(later, s[:, :HD], NEG),
                        s[:, HD:WIN - HD],
                        jnp.where(later, NEG, s[:, WIN - HD:]),
                    ],
                    axis=1,
                )
                s = jnp.where(real, s, NEG)
                peak = jnp.max(s, axis=1, keepdims=True)
                e = jnp.exp2((s - peak) * EXP_SCALE)
                probs = (e * (1.0 / jnp.sum(e, axis=1, keepdims=True))).astype(BF16)
                o = jnp.dot(probs, vals, preferred_element_type=F32).astype(BF16)
                o_ref[pl.ds(r0, HD), (j - 1) * 256:(j - 1) * 256 + HD] = o[:HD]
                o_ref[pl.ds(r0, HD), (j - 1) * 256 + HD:j * 256] = o[HD:]
                return carry

            lax.fori_loop(0, TOK // HD, block, 0, unroll=True)
        plan.add(f"a{j}", window_in + [f"done:f{h}{j}" for h in range(2)], 3.0, 7 + j, go)

    kvf = kvb.reshape(6 * TOK, 2 * HD)
    for j in range(1, NCH):
        attend(j)

    plan.emit(start)
    body.total = plan.total

    for cp in started:
        cp.wait_send()
    for t in range(2):
        for m in range(NSUB):
            for k in range(2):
                ref = hpiece(t, y, m)
                remote(ref, ref, hy_s.at[t, m, k], hy_r.at[t, m, k], yup).wait_send()

    for m in range(3, NSUB):
        remote(xv.at[hrows(m)], hid.at[first_t, y, hrows(m)], hx_s.at[0, m], hx_r.at[first_t, m], first_to).wait_send()

    @pl.when(inner)
    def _():
        for m in range(NSUB):
            ref = hpiece(0, y, m)
            remote(ref, ref, hx_s.at[1, m], hx_r.at[0, m], side).wait_send()


def shards(hidden_states, norm_gain, qkv_weight, block_mask):
    ci = lax.axis_index("ctx")
    position = (ci * TOK + jnp.arange(TOK, dtype=jnp.int32)).astype(F32)
    inverse = jnp.power(F32(500000.0), -(jnp.arange(0, HD, 2).astype(F32) / HD))
    angles = position[:, None] * inverse[None, :]
    cosine, sine = jnp.cos(angles), jnp.sin(angles)
    gain = norm_gain.astype(F32).reshape(8, WID)
    any_ = pl.BlockSpec(memory_space=pl.ANY)
    hbm = pl.BlockSpec(memory_space=pltpu.HBM)
    dma = pltpu.SemaphoreType.DMA
    result = pl.pallas_call(
        body,
        out_shape=jax.ShapeDtypeStruct((TOK, 1024), BF16),
        in_specs=[
            hbm, pl.BlockSpec(memory_space=pltpu.VMEM), hbm, pl.BlockSpec(memory_space=pltpu.SMEM), any_, any_,
        ],
        out_specs=pl.BlockSpec(memory_space=pltpu.VMEM),
        scratch_shapes=[
            pltpu.VMEM((TOK, WID), BF16),
            pltpu.VMEM((ROWS, 1280), BF16),
            pltpu.VMEM((TOK, HD // 2), F32),
            pltpu.VMEM((TOK, HD // 2), F32),
            pltpu.VMEM((TOK, HD), F32),
            pltpu.VMEM((TOK, HD), F32),
            pltpu.VMEM((2, 4, TOK, WID), BF16),
            pltpu.VMEM((2, TOK, KH), BF16),
            pltpu.VMEM((NCH, KH, 256), BF16),
            pltpu.VMEM((NCH, TOK, 256), F32),
            pltpu.VMEM((NCH, TOK, 256), F32),
            pltpu.VMEM((NCH, TOK, 256), F32),
            pltpu.VMEM((4, TOK, 256), BF16),
            pltpu.VMEM((6, TOK, 256), BF16),
            pltpu.VMEM((8, 8, TOK), F32),
            pltpu.VMEM((2, 8, TOK), F32),
            pltpu.VMEM((2, TOK, HD), F32),
            dma((5,)),
            dma((NCH, 2, 4)), dma((NCH, 2, 4)),
            dma((NCH, 8)), dma((NCH, 8)),
            dma((2, NSUB)), dma((2, NSUB)),
            dma((2, NSUB, 3)), dma((2, NSUB, 3)),
            dma((7,)), dma((7,)),
            dma((1,)), dma((1,)),
            dma((NCH, 4)), dma((NCH, 4)),
            dma((5, len(KGROUPS))), dma((5, len(KGROUPS))),
        ],
        compiler_params=pltpu.CompilerParams(
            collective_id=0, has_side_effects=True, vmem_limit_bytes=52 * 2**20
        ),
        cost_estimate=pl.CostEstimate(flops=12 * 10**9, bytes_accessed=3 * 10**6, transcendentals=6 * 10**6),
    )(
        hidden_states, gain, qkv_weight.reshape(ROWS, 1280), block_mask.reshape(2, 10), cosine, sine,
    )
    return result.reshape(TOK, 1, 1024)


def solution(mesh):
    return jax.shard_map(
        shards,
        mesh=mesh,
        in_specs=(P("ctx", "fsdp"), P(), P("ctx", "fsdp", None), P("ctx", "fsdp", None)),
        out_specs=P("ctx", "fsdp", None),
        check_vma=False,
    )
```

```python
import jax
import jax.numpy as jnp
from jax import lax
from jax.experimental import pallas as pl
from jax.experimental.pallas import tpu as pltpu
from jax.sharding import PartitionSpec as P

MESH = pl.DeviceIdType.MESH
F32 = jnp.float32
BF16 = jnp.bfloat16
HD = 128
TOK = 384
WID = 1024
KH = 4096
ROWS = 256
NCH = 5
SUB = 48
NSUB = TOK // SUB
HALF = TOK // 2
STEPS = 4
WIN = STEPS * TOK + HD
NEG = -1e30
BACK = (2, 2, 2)
EARLY = 0
OWN = 1
AHEAD = 3
TGROUPS = (((0, 2), (2, 4), (4, 6), (6, 8)), ((0, 4), (4, 8)))
QGROUPS = ((0, 4), (4, 8))
KGROUPS = ((0, 4), (4, 6), (6, 8))
EXP_SCALE = HD ** (-0.5) * 1.4426950408889634


class Plan:
    def __init__(self):
        self.tasks = []
        self.waits = {}

    def token(self, name, wait=None):
        self.waits[name] = wait
        return name

    def add(self, name, deps, dur, prio, emit, sends=()):
        self.tasks.append((name, list(deps), dur, prio, emit, list(sends)))

    def order(self, start):
        ready = {name: 0.0 for name in start}
        free = {}
        now = 0.0
        left = list(self.tasks)
        done = []
        while left:
            best = None
            soonest = None
            for task in left:
                if all(d in ready for d in task[1]):
                    at = max([ready[d] for d in task[1]], default=0.0)
                    if at <= now:
                        if best is None or task[3] < best[3]:
                            best = task
                    elif soonest is None or at < soonest:
                        soonest = at
            if best is None:
                now = soonest
                continue
            left.remove(best)
            done.append(best)
            now += best[2]
            ready["done:" + best[0]] = now
            for link, dur, lat, token in best[5]:
                begin = max(now, free.get(link, 0.0))
                free[link] = begin + dur
                ready[token] = begin + dur + lat
        self.total = now
        return done

    def emit(self, start):
        waited = set()
        for name, deps, _, _, emit, _ in self.order(start):
            for d in deps:
                if d not in waited and self.waits.get(d) is not None:
                    self.waits[d]()
                waited.add(d)
            emit()


def body(
    x_hbm, g_ref, w_hbm, mask_ref, cos_hbm, sin_hbm, o_ref,
    xv, wv, half_c, half_n, cosv, sinv, hid, nrm, wts, part, got, acc, qbuf, kvb, sq, tot, rs,
    in_s, wz_s, wz_r, ws_s, ws_r, hx_s, hx_r, hy_s, hy_r, sq_s, sq_r, tx_s, tx_r,
    pr_s, pr_r, kv_s, kv_r,
):
    ci = lax.axis_index("ctx")
    fi = lax.axis_index("fsdp")
    xh, z, c = ci // 16, (ci // 2) % 8, ci % 2
    xl, y = fi // 4, fi % 4
    inner = xh != xl

    def dev(xh_, z_, c_, xl_, y_):
        return (xh_ * 16 + z_ * 2 + c_, xl_ * 4 + y_)

    up = dev(xh, (z + 1) % 8, c, xl, y)
    down = dev(xh, (z + 7) % 8, c, xl, y)
    sib = dev(xh, z, 1 - c, xl, y)
    far = dev(1 - xh, z, c, xl, y)
    cross = dev(1 - xh, z, c, 1 - xl, y)
    side = dev(xh, z, c, 1 - xl, y)
    yup = dev(xh, z, c, xl, (y + 1) % 4)
    ydown = dev(xh, z, c, xl, (y + 3) % 4)
    after = ((ci + 2) % 32, fi)
    before = ((ci + 30) % 32, fi)
    peers = [(ci, (fi + k) % 8) for k in range(1, 8)]

    started = []

    def remote(src, dst, s, r, to):
        return pltpu.make_async_remote_copy(
            src_ref=src, dst_ref=dst, send_sem=s, recv_sem=r, device_id=to, device_id_type=MESH
        )

    def send(*args):
        cp = remote(*args)
        cp.start()
        started.append(cp)

    load_w = pltpu.make_async_copy(w_hbm, wv, in_s.at[0])
    load_x = pltpu.make_async_copy(x_hbm, xv, in_s.at[1])
    load_c = pltpu.make_async_copy(cos_hbm, half_c, in_s.at[2])
    load_n = pltpu.make_async_copy(sin_hbm, half_n, in_s.at[3])
    load_h = pltpu.make_async_copy(x_hbm, hid.at[1, y], in_s.at[4])
    load_w.start()
    load_x.start()
    load_c.start()
    load_n.start()

    @pl.when(jnp.logical_not(inner))
    def _():
        load_h.start()

    barrier = pltpu.get_barrier_semaphore()
    greeted = peers + [far, cross, up, down, sib, after, before]
    for d in greeted:
        pl.semaphore_signal(barrier, inc=1, device_id=d, device_id_type=MESH)

    load_w.wait()
    own_piece = z * 2 + c

    def piece(j, idx):
        return wts.at[j, pl.ds(pl.multiple_of(idx * ROWS, ROWS), ROWS)]

    for j in range(NCH):
        for half in range(2):
            head = 8 + half if j == 0 else 2 * (j - 1) + half
            for rb in range(2):
                keep = mask_ref[rb, head].astype(F32)
                block = wv[rb * 128:(rb + 1) * 128, head * 128:(head + 1) * 128].astype(F32)
                wts[j, pl.ds(pl.multiple_of(own_piece * ROWS + rb * 128, 128), 128), half * 128:(half + 1) * 128] = (
                    block * keep
                ).astype(BF16)
    load_x.wait()

    lanes = jnp.zeros((TOK, 128), F32)
    for k in range(WID // 128):
        v = xv[:, k * 128:(k + 1) * 128].astype(F32)
        lanes = lanes + v * v
    sums = lax.dot_general(
        jnp.ones((8, 128), F32), lanes, (((1,), (1,)), ((), ())),
        precision=lax.Precision.HIGHEST, preferred_element_type=F32,
    )
    sq[fi] = sums
    pl.semaphore_wait(barrier, len(greeted))
    for k in range(1, 8):
        send(sq.at[fi], sq.at[fi], sq_s.at[k - 1], sq_r.at[k - 1], peers[k - 1])


    def hrows(m):
        return pl.ds(m * SUB, SUB)

    first_to = (
        jnp.where(inner, cross[0], side[0]),
        jnp.where(inner, cross[1], side[1]),
    )
    first_t = jnp.where(inner, 0, 1)

    def first_send(m):
        send(xv.at[hrows(m)], hid.at[first_t, y, hrows(m)], hx_s.at[0, m], hx_r.at[first_t, m], first_to)

    def own_send(j):
        src = piece(j, own_piece)
        send(src, src, wz_s.at[j, 0, 0], wz_r.at[j, 0, 0], up)
        send(src, src, wz_s.at[j, 1, 0], wz_r.at[j, 1, 0], down)
        send(src, src, ws_s.at[j, 0], ws_r.at[j, 0], sib)

    first_send(0)
    own_send(0)
    first_send(1)
    for j in range(1, BACK[2]):
        own_send(j)
    first_send(2)

    @pl.when(jnp.logical_not(inner))
    def _():
        load_h.wait()

    plan = Plan()
    start = []

    def at(step):
        return ((z + 8 + step) % 8) * 2 + c

    pz, lz = 3.1, 2.0

    def wait_w(j, way, d):
        def go():
            if d < 3:
                ref = piece(j, at(-(d + 1) if way == 0 else d + 1))
            else:
                ref = wts.at[j, pl.ds(pl.multiple_of(at(4) * ROWS + way * 128, 128), 128)]
            remote(ref, ref, wz_s.at[j, way, d], wz_r.at[j, way, d], sib).wait_recv()
        return go

    def wait_s(j, k):
        def go():
            ref = wts.at[j, pl.ds(0, ROWS)]
            remote(ref, ref, ws_s.at[j, k], ws_r.at[j, k], sib).wait_recv()
        return go

    for j in range(NCH):
        for way in range(2):
            for d in range(4):
                plan.token(f"w{j}{way}{d}", wait_w(j, way, d))
        for k in range(8):
            plan.token(f"s{j}{k}", wait_s(j, k))

    def own_task(j):
        plan.add(
            f"own{j}", [f"done:w{j-BACK[0]}{way}{BACK[1]}f" for way in range(2)] if j >= BACK[2] else [], 0.3, 0,
            (lambda: own_send(j)) if j >= BACK[2] else (lambda: None),
            [("zu", pz, lz, f"w{j}00"), ("zd", pz, lz, f"w{j}10"), ("cc", 0.6, 1.0, f"s{j}0")],
        )

    def fwd_task(j, way, d):
        def go():
            idx = at(-(d + 1) if way == 0 else d + 1)
            to = up if way == 0 else down
            if d < 2:
                src = piece(j, idx)
            else:
                src = wts.at[j, pl.ds(pl.multiple_of(idx * ROWS + way * 128, 128), 128)]
            send(src, src, wz_s.at[j, way, d + 1], wz_r.at[j, way, d + 1], to)
            src = piece(j, idx)
            k = 1 + way * 3 + d
            send(src, src, ws_s.at[j, k], ws_r.at[j, k], sib)
        link = "zu" if way == 0 else "zd"
        plan.add(
            f"w{j}{way}{d}f", [f"w{j}{way}{d}"], 0.2, 1, go,
            [(link, pz if d < 2 else pz / 2, lz, f"w{j}{way}{d+1}"), ("cc", 0.6, 1.0, f"s{j}{1+way*3+d}")],
        )

    def last_task(j):
        def go():
            src = piece(j, at(4))
            send(src, src, ws_s.at[j, 7], ws_r.at[j, 7], sib)
        plan.add(f"w{j}l", [f"w{j}03", f"w{j}13"], 0.1, 1, go, [("cc", 0.6, 1.0, f"s{j}7")])

    for j in range(NCH):
        own_task(j)
        for way in range(2):
            for d in range(3):
                fwd_task(j, way, d)
        last_task(j)
    chunk_in = [
        [f"s{j}{k}" for k in range(8)]
        + [f"done:w{j}{way}{d}f" for way in range(2) for d in range(3)]
        + [f"done:w{j}l"]
        for j in range(NCH)
    ]

    ph, lh = 2.35, 2.0

    def hpiece(t, yy, m):
        return hid.at[t, yy, hrows(m)]

    def wait_hx(t, m):
        ref = hpiece(t, y, m)
        remote(ref, ref, hx_s.at[0, m], hx_r.at[t, m], sib).wait_recv()

    def y_sends(t, m):
        ref = hpiece(t, y, m)
        send_when.append(remote(ref, ref, hy_s.at[t, m, 0], hy_r.at[t, m, 0], yup))
        send_when[-1].start()
        send_when.append(remote(ref, ref, hy_s.at[t, m, 1], hy_r.at[t, m, 1], ydown))
        send_when[-1].start()

    send_when = []
    y_links = lambda t, m: [("yu", ph, lh, f"y{t}{m}0"), ("yd", ph, lh, f"y{t}{m}1")]
    seq = [(0, m) for m in range(EARLY)] + [(1, m) for m in range(OWN)] + [(0, m) for m in range(EARLY, NSUB)] + [(1, m) for m in range(OWN, NSUB)]
    rank = {tm: n for n, tm in enumerate(seq)}

    def more(m):
        if m + 3 < NSUB:
            src = xv.at[hrows(m + 3)]
            remote(src, hid.at[first_t, y, hrows(m + 3)], hx_s.at[0, m + 3], hx_r.at[first_t, m + 3], first_to).start()

    def x_in(m):
        def go():
            @pl.when(inner)
            def _():
                wait_hx(0, m)
                ref = hpiece(0, y, m)
                remote(ref, ref, hx_s.at[1, m], hx_r.at[0, m], side).start()
                more(m)
        plan.add(
            f"xi0{m}", [f"xa0{m}"], 0.1, 2, go,
            [("xo", ph, lh, f"xb0{m}")] + ([("xi", ph, lh, f"xa0{m+3}")] if m + 3 < NSUB else []),
        )

    def x_out(m):
        def go():
            @pl.when(jnp.logical_not(inner))
            def _():
                wait_hx(0, m)
                more(m)
        plan.add(
            f"xo0{m}", [f"xb0{m}"], 0.1, 2, go,
            [("xs", ph, lh, f"xc1{m+3}")] if m + 3 < NSUB else [],
        )

    def x_own(m):
        def go():
            @pl.when(inner)
            def _():
                wait_hx(1, m)
        plan.add(f"xo1{m}", [f"xc1{m}"], 0.1, 3, go)

    def y_own(t, m):
        n = rank[(t, m)]
        deps = [f"done:xo{t}{m}"] + ([f"done:xi{t}{m}"] if t == 0 else [])
        if n >= AHEAD:
            deps.append("done:yf%d%d" % seq[n - AHEAD])
        plan.add(f"ys{t}{m}", deps, 0.1, 1.5, lambda: y_sends(t, m), y_links(t, m))

    plan.add(
        "first", [], 0.5, -1, lambda: None,
        [("xi", ph, lh, f"xa0{m}") for m in range(3)] + [("xs", ph, lh, f"xc1{m}") for m in range(3)],
    )
    for m in range(NSUB):
        x_in(m)
        x_out(m)
        x_own(m)
        for t in range(2):
            y_own(t, m)

    def wait_y(t, m, k):
        def go():
            idx = (y + 3) % 4 if k == 0 else (y + 1) % 4 if k == 1 else (y + 2) % 4
            ref = hpiece(t, idx, m)
            remote(ref, ref, hy_s.at[t, m, k], hy_r.at[t, m, k], sib).wait_recv()
        return go

    def y_task(t, m):
        way = m % 2
        for k in range(3):
            plan.token(f"y{t}{m}{k}", wait_y(t, m, k))

        def go():
            ref = hpiece(t, (y + 3) % 4 if way == 0 else (y + 1) % 4, m)
            send(ref, ref, hy_s.at[t, m, 2], hy_r.at[t, m, 2], yup if way == 0 else ydown)
        plan.add(
            f"yf{t}{m}", [f"y{t}{m}{way}"], 0.1, 2, go, [("yu" if way == 0 else "yd", ph, lh, f"y{t}{m}2")]
        )

    def wait_sq(k):
        def go():
            remote(sq.at[0], sq.at[0], sq_s.at[k], sq_r.at[k], sib).wait_recv()
        return go

    def spread(which, rows8):
        inv = lax.rsqrt(rows8 * (1.0 / 8192.0) + 1e-05)
        rs[which] = lax.dot_general(
            inv, jnp.full((8, 128), 0.125, F32), (((0,), (0,)), ((), ())),
            precision=lax.Precision.HIGHEST, preferred_element_type=F32,
        )

    def total():
        rows8 = sq[0]
        for k in range(1, 8):
            rows8 = rows8 + sq[k]
        tot[1] = rows8
        send(tot.at[1], tot.at[0], tx_s.at[0], tx_r.at[0], far)
        spread(1, rows8)

    def wait_tx():
        remote(tot.at[1], tot.at[0], tx_s.at[0], tx_r.at[0], far).wait_recv()

    plan.token("tx", wait_tx)
    for k in range(7):
        start.append(plan.token(f"sq{k}", wait_sq(k)))
    plan.add("sqa", ["done:first"], 3.0, 0, lambda: None)
    plan.add("total", [f"sq{k}" for k in range(7)] + ["done:sqa"], 0.5, 1, total, [("none", 0, 2.5, "tx")])
    plan.add("other", ["tx"], 0.5, 1, lambda: spread(0, tot[0]))

    def norm_task(t, m, step, deps):
        def go():
            yy = (y + step) % 4
            gain = g_ref[pl.ds(xh * 4 + yy, 1), :]
            scale = rs[t, m * SUB:(m + 1) * SUB, :]
            for k in range(WID // 128):
                v = hid[t, yy, m * SUB:(m + 1) * SUB, k * 128:(k + 1) * 128].astype(F32)
                v = v * scale * gain[:, k * 128:(k + 1) * 128]
                nrm[t, m * SUB:(m + 1) * SUB, pl.ds(pl.multiple_of(yy * WID + k * 128, 128), 128)] = v.astype(BF16)
        plan.add(f"n{t}{m}{step}", deps + ["done:other" if t == 0 else "done:total"], 0.05, 4 + rank[(t, m)] * 0.01, go)

    for t in range(2):
        for m in range(NSUB):
            y_task(t, m)
            norm_task(t, m, 0, [f"done:xo{t}{m}"] + ([f"done:xi{t}{m}"] if t == 0 else []))
            norm_task(t, m, 3, [f"y{t}{m}0"])
            norm_task(t, m, 1, [f"y{t}{m}1"])
            norm_task(t, m, 2, [f"y{t}{m}2"])

    def product(t, lo, hi, j):
        return jnp.dot(nrm[t, lo * SUB:hi * SUB, :], wts[j], preferred_element_type=F32)

    def sent(j):
        return TGROUPS[0] if j < 2 else TGROUPS[1]

    def sent_rows(j, h):
        lo, hi = sent(j)[h]
        return pl.ds(lo * SUB, (hi - lo) * SUB)

    def wait_pr(j, h):
        def go():
            ref = got.at[j, sent_rows(j, h)]
            remote(ref, ref, pr_s.at[j, h], pr_r.at[j, h], far).wait_recv()
        return go

    def other_task(h, j):
        lo, hi = sent(j)[h]

        def go():
            rows = sent_rows(j, h)
            part[j, rows] = product(0, lo, hi, j)
            send(part.at[j, rows], got.at[j, rows], pr_s.at[j, h], pr_r.at[j, h], far)
        plan.token(f"p{j}{h}", wait_pr(j, h))
        deps = [f"done:n0{m}{s}" for m in range(lo, hi) for s in range(4)]
        plan.add(
            f"m0{h}{j}", deps + chunk_in[j] + (["done:kb%d" % (len(KGROUPS) - 1)] if j == NCH - 1 else []), 1.0 if hi - lo > 2 else 0.7, 5 + j * 0.1 + h * 0.01, go,
            [("xp", 1.2 * (hi - lo), 3.0, f"p{j}{h}")],
        )

    def rotated(u, rows):
        return u * cosv[rows, :] + pltpu.roll(u, 64, 1) * sinv[rows, :]

    def groups(j):
        return KGROUPS if j == 0 else QGROUPS

    def own_product(h, j):
        lo, hi = groups(j)[h]

        def go():
            acc[j, pl.ds(lo * SUB, (hi - lo) * SUB)] = product(1, lo, hi, j)
        deps = [f"done:n1{m}{s}" for m in range(lo, hi) for s in range(4)]
        plan.add(f"m1{h}{j}", deps + chunk_in[j], 1.0 if hi - lo > 2 else 0.7, (4.4 if j == 0 else 6) + j * 0.1 + h * 0.01, go)

    def kv_send(blk_from, blk_to, h, k, to):
        lo, hi = KGROUPS[h]
        rows = pl.ds(lo * SUB, (hi - lo) * SUB)
        send(kvb.at[blk_from, rows], kvb.at[blk_to, rows], kv_s.at[k, h], kv_r.at[k, h], to)

    def kv_time(h):
        return 0.55 * (KGROUPS[h][1] - KGROUPS[h][0])

    def finish(h, j):
        lo, hi = groups(j)[h]

        def go():
            rows = pl.ds(lo * SUB, (hi - lo) * SUB)
            u = acc[j, rows] + got[j, rows]
            left, right = u[:, :HD], u[:, HD:]
            if j == 0:
                kvb[4 + c, rows, 0:HD] = rotated(left, rows).astype(BF16)
                kvb[4 + c, rows, HD:2 * HD] = right.astype(BF16)
                kv_send(4 + c, 2 + c, h, 0, after)
                kv_send(4 + c, 4 + c, h, 2, sib)
            else:
                qbuf[j - 1, rows, 0:HD] = rotated(left, rows).astype(BF16)
                qbuf[j - 1, rows, HD:2 * HD] = rotated(right, rows).astype(BF16)
        sends = [("zu", kv_time(h), 2.0, f"k0{h}"), ("cc", 0.3, 1.0, f"k2{h}")] if j == 0 else []
        parts = [p for p, (a, b) in enumerate(sent(j)) if a < hi and b > lo]
        plan.add(
            f"f{h}{j}", [f"done:m1{h}{j}", "done:rope"] + [f"p{j}{p}" for p in parts], 0.2, 4.5 + j * 0.1, go, sends
        )

    def rope():
        load_c.wait()
        load_n.wait()
        cosv[...] = jnp.concatenate([half_c[...], half_c[...]], axis=1)
        sinv[...] = jnp.concatenate([-half_n[...], half_n[...]], axis=1)

    plan.add("rope", ["done:other"], 0.5, 3.5, rope)

    def wait_kv(k, h):
        def go():
            ref = kvb.at[0, pl.ds(0, (KGROUPS[h][1] - KGROUPS[h][0]) * SUB)]
            remote(ref, ref, kv_s.at[k, h], kv_r.at[k, h], sib).wait_recv()
        return go

    for h in range(len(KGROUPS)):
        for k in range(5):
            plan.token(f"k{k}{h}", wait_kv(k, h))

        def pass_one(h=h):
            kv_send(2 + c, c, h, 1, after)
            kv_send(2 + c, 2 + c, h, 3, sib)

        def pass_two(h=h):
            kv_send(c, c, h, 4, sib)

        plan.add(f"ka{h}", [f"k0{h}"], 0.1, 1, pass_one, [("zu", kv_time(h), 2.0, f"k1{h}"), ("cc", 0.3, 1.0, f"k3{h}")])
        plan.add(f"kb{h}", [f"k1{h}"], 0.1, 1, pass_two, [("cc", 0.3, 1.0, f"k4{h}")])
    for j in range(NCH):
        for h in range(len(sent(j))):
            other_task(h, j)
        for h in range(len(groups(j))):
            own_product(h, j)
            finish(h, j)
    ngk = len(KGROUPS)
    window_in = [f"k{k}{h}" for k in (2, 3, 4) for h in range(ngk)] + [f"done:kb{h}" for h in range(ngk)] + [f"done:f{h}0" for h in range(ngk)]

    def attend(j):
        def go():
            row = lax.broadcasted_iota(jnp.int32, (2 * HD, HD), 0)
            col = lax.broadcasted_iota(jnp.int32, (2 * HD, HD), 1)
            later = col > row % HD
            key_at = lax.broadcasted_iota(jnp.int32, (1, WIN), 1)

            def block(b, carry):
                r0 = pl.multiple_of(b * HD, HD)
                k0 = pl.multiple_of(c * TOK + b * HD, HD)
                keys = kvf[pl.ds(k0, WIN), 0:HD]
                vals = kvf[pl.ds(k0, WIN), HD:2 * HD]
                real = key_at >= (STEPS - ci) * TOK - b * HD
                q = jnp.concatenate(
                    [qbuf[j - 1, pl.ds(r0, HD), 0:HD], qbuf[j - 1, pl.ds(r0, HD), HD:2 * HD]], axis=0
                )
                s = lax.dot_general(q, keys, (((1,), (1,)), ((), ())), preferred_element_type=F32)
                s = jnp.concatenate(
                    [
                        jnp.where(later, s[:, :HD], NEG),
                        s[:, HD:WIN - HD],
                        jnp.where(later, NEG, s[:, WIN - HD:]),
                    ],
                    axis=1,
                )
                s = jnp.where(real, s, NEG)
                peak = jnp.max(s, axis=1, keepdims=True)
                e = jnp.exp2((s - peak) * EXP_SCALE)
                probs = (e * (1.0 / jnp.sum(e, axis=1, keepdims=True))).astype(BF16)
                o = jnp.dot(probs, vals, preferred_element_type=F32).astype(BF16)
                o_ref[pl.ds(r0, HD), (j - 1) * 256:(j - 1) * 256 + HD] = o[:HD]
                o_ref[pl.ds(r0, HD), (j - 1) * 256 + HD:j * 256] = o[HD:]
                return carry

            lax.fori_loop(0, TOK // HD, block, 0, unroll=True)
        plan.add(f"a{j}", window_in + [f"done:f{h}{j}" for h in range(2)], 3.0, 7 + j, go)

    kvf = kvb.reshape(6 * TOK, 2 * HD)
    for j in range(1, NCH):
        attend(j)

    plan.emit(start)
    body.total = plan.total

    for cp in started:
        cp.wait_send()
    for t in range(2):
        for m in range(NSUB):
            for k in range(2):
                ref = hpiece(t, y, m)
                remote(ref, ref, hy_s.at[t, m, k], hy_r.at[t, m, k], yup).wait_send()

    for m in range(3, NSUB):
        remote(xv.at[hrows(m)], hid.at[first_t, y, hrows(m)], hx_s.at[0, m], hx_r.at[first_t, m], first_to).wait_send()

    @pl.when(inner)
    def _():
        for m in range(NSUB):
            ref = hpiece(0, y, m)
            remote(ref, ref, hx_s.at[1, m], hx_r.at[0, m], side).wait_send()


def shards(hidden_states, norm_gain, qkv_weight, block_mask):
    ci = lax.axis_index("ctx")
    position = (ci * TOK + jnp.arange(TOK, dtype=jnp.int32)).astype(F32)
    inverse = jnp.power(F32(500000.0), -(jnp.arange(0, HD, 2).astype(F32) / HD))
    angles = position[:, None] * inverse[None, :]
    cosine, sine = jnp.cos(angles), jnp.sin(angles)
    gain = norm_gain.astype(F32).reshape(8, WID)
    any_ = pl.BlockSpec(memory_space=pl.ANY)
    hbm = pl.BlockSpec(memory_space=pltpu.HBM)
    dma = pltpu.SemaphoreType.DMA
    result = pl.pallas_call(
        body,
        out_shape=jax.ShapeDtypeStruct((TOK, 1024), BF16),
        in_specs=[
            hbm, pl.BlockSpec(memory_space=pltpu.VMEM), hbm, pl.BlockSpec(memory_space=pltpu.SMEM), any_, any_,
        ],
        out_specs=pl.BlockSpec(memory_space=pltpu.VMEM),
        scratch_shapes=[
            pltpu.VMEM((TOK, WID), BF16),
            pltpu.VMEM((ROWS, 1280), BF16),
            pltpu.VMEM((TOK, HD // 2), F32),
            pltpu.VMEM((TOK, HD // 2), F32),
            pltpu.VMEM((TOK, HD), F32),
            pltpu.VMEM((TOK, HD), F32),
            pltpu.VMEM((2, 4, TOK, WID), BF16),
            pltpu.VMEM((2, TOK, KH), BF16),
            pltpu.VMEM((NCH, KH, 256), BF16),
            pltpu.VMEM((NCH, TOK, 256), F32),
            pltpu.VMEM((NCH, TOK, 256), F32),
            pltpu.VMEM((NCH, TOK, 256), F32),
            pltpu.VMEM((4, TOK, 256), BF16),
            pltpu.VMEM((6, TOK, 256), BF16),
            pltpu.VMEM((8, 8, TOK), F32),
            pltpu.VMEM((2, 8, TOK), F32),
            pltpu.VMEM((2, TOK, HD), F32),
            dma((5,)),
            dma((NCH, 2, 4)), dma((NCH, 2, 4)),
            dma((NCH, 8)), dma((NCH, 8)),
            dma((2, NSUB)), dma((2, NSUB)),
            dma((2, NSUB, 3)), dma((2, NSUB, 3)),
            dma((7,)), dma((7,)),
            dma((1,)), dma((1,)),
            dma((NCH, 4)), dma((NCH, 4)),
            dma((5, len(KGROUPS))), dma((5, len(KGROUPS))),
        ],
        compiler_params=pltpu.CompilerParams(
            collective_id=0, has_side_effects=True, vmem_limit_bytes=52 * 2**20
        ),
        cost_estimate=pl.CostEstimate(flops=12 * 10**9, bytes_accessed=3 * 10**6, transcendentals=6 * 10**6),
    )(
        hidden_states, gain, qkv_weight.reshape(ROWS, 1280), block_mask.reshape(2, 10), cosine, sine,
    )
    return result.reshape(TOK, 1, 1024)


def solution(mesh):
    return jax.shard_map(
        shards,
        mesh=mesh,
        in_specs=(P("ctx", "fsdp"), P(), P("ctx", "fsdp", None), P("ctx", "fsdp", None)),
        out_specs=P("ctx", "fsdp", None),
        check_vma=False,
    )
```

```python
import jax
import jax.numpy as jnp
from jax import lax
from jax.experimental import pallas as pl
from jax.experimental.pallas import tpu as pltpu
from jax.sharding import PartitionSpec as P

MESH = pl.DeviceIdType.MESH
F32 = jnp.float32
BF16 = jnp.bfloat16
HD = 128
TOK = 384
WID = 1024
KH = 4096
ROWS = 256
NCH = 5
SUB = 48
NSUB = TOK // SUB
HALF = TOK // 2
STEPS = 4
WIN = STEPS * TOK + HD
NEG = -1e30
BACK = (2, 2, 2)
EARLY = 0
OWN = 1
AHEAD = 3
TGROUPS = (((0, 2), (2, 4), (4, 6), (6, 8)), ((0, 4), (4, 8)))
QGROUPS = ((0, 4), (4, 8))
KGROUPS = ((0, 4), (4, 6), (6, 8))
EXP_SCALE = HD ** (-0.5) * 1.4426950408889634


class Plan:
    def __init__(self):
        self.tasks = []
        self.waits = {}

    def token(self, name, wait=None):
        self.waits[name] = wait
        return name

    def add(self, name, deps, dur, prio, emit, sends=()):
        self.tasks.append((name, list(deps), dur, prio, emit, list(sends)))

    def order(self, start):
        ready = {name: 0.0 for name in start}
        free = {}
        now = 0.0
        left = list(self.tasks)
        done = []
        while left:
            best = None
            soonest = None
            for task in left:
                if all(d in ready for d in task[1]):
                    at = max([ready[d] for d in task[1]], default=0.0)
                    if at <= now:
                        if best is None or task[3] < best[3]:
                            best = task
                    elif soonest is None or at < soonest:
                        soonest = at
            if best is None:
                now = soonest
                continue
            left.remove(best)
            done.append(best)
            now += best[2]
            ready["done:" + best[0]] = now
            for link, dur, lat, token in best[5]:
                begin = max(now, free.get(link, 0.0))
                free[link] = begin + dur
                ready[token] = begin + dur + lat
        self.total = now
        return done

    def emit(self, start):
        waited = set()
        for name, deps, _, _, emit, _ in self.order(start):
            for d in deps:
                if d not in waited and self.waits.get(d) is not None:
                    self.waits[d]()
                waited.add(d)
            emit()


def body(
    x_hbm, g_ref, w_hbm, mask_ref, cos_hbm, sin_hbm, o_ref,
    xv, wv, half_c, half_n, cosv, sinv, hid, nrm, wts, part, got, acc, qbuf, kvb, sq, tot, rs,
    in_s, wz_s, wz_r, ws_s, ws_r, hx_s, hx_r, hy_s, hy_r, sq_s, sq_r, tx_s, tx_r,
    pr_s, pr_r, kv_s, kv_r,
):
    ci = lax.axis_index("ctx")
    fi = lax.axis_index("fsdp")
    xh, z, c = ci // 16, (ci // 2) % 8, ci % 2
    xl, y = fi // 4, fi % 4
    inner = xh != xl

    def dev(xh_, z_, c_, xl_, y_):
        return (xh_ * 16 + z_ * 2 + c_, xl_ * 4 + y_)

    up = dev(xh, (z + 1) % 8, c, xl, y)
    down = dev(xh, (z + 7) % 8, c, xl, y)
    sib = dev(xh, z, 1 - c, xl, y)
    far = dev(1 - xh, z, c, xl, y)
    cross = dev(1 - xh, z, c, 1 - xl, y)
    side = dev(xh, z, c, 1 - xl, y)
    yup = dev(xh, z, c, xl, (y + 1) % 4)
    ydown = dev(xh, z, c, xl, (y + 3) % 4)
    after = ((ci + 2) % 32, fi)
    before = ((ci + 30) % 32, fi)
    peers = [(ci, (fi + k) % 8) for k in range(1, 8)]

    started = []

    def remote(src, dst, s, r, to):
        return pltpu.make_async_remote_copy(
            src_ref=src, dst_ref=dst, send_sem=s, recv_sem=r, device_id=to, device_id_type=MESH
        )

    def send(*args):
        cp = remote(*args)
        cp.start()
        started.append(cp)

    load_w = pltpu.make_async_copy(w_hbm, wv, in_s.at[0])
    load_x = pltpu.make_async_copy(x_hbm, xv, in_s.at[1])
    load_c = pltpu.make_async_copy(cos_hbm, half_c, in_s.at[2])
    load_n = pltpu.make_async_copy(sin_hbm, half_n, in_s.at[3])
    load_h = pltpu.make_async_copy(x_hbm, hid.at[1, y], in_s.at[4])
    load_w.start()
    load_x.start()
    load_c.start()
    load_n.start()

    @pl.when(jnp.logical_not(inner))
    def _():
        load_h.start()

    barrier = pltpu.get_barrier_semaphore()
    greeted = peers + [far, cross, up, down, sib, after, before]
    for d in greeted:
        pl.semaphore_signal(barrier, inc=1, device_id=d, device_id_type=MESH)

    load_w.wait()
    own_piece = z * 2 + c

    def piece(j, idx):
        return wts.at[j, pl.ds(pl.multiple_of(idx * ROWS, ROWS), ROWS)]

    for j in range(NCH):
        for half in range(2):
            head = 8 + half if j == 0 else 2 * (j - 1) + half
            for rb in range(2):
                keep = mask_ref[rb, head].astype(F32)
                block = wv[rb * 128:(rb + 1) * 128, head * 128:(head + 1) * 128].astype(F32)
                wts[j, pl.ds(pl.multiple_of(own_piece * ROWS + rb * 128, 128), 128), half * 128:(half + 1) * 128] = (
                    block * keep
                ).astype(BF16)
    load_x.wait()

    lanes = jnp.zeros((TOK, 128), F32)
    for k in range(WID // 128):
        v = xv[:, k * 128:(k + 1) * 128].astype(F32)
        lanes = lanes + v * v
    sums = lax.dot_general(
        jnp.ones((8, 128), F32), lanes, (((1,), (1,)), ((), ())),
        precision=lax.Precision.HIGHEST, preferred_element_type=F32,
    )
    sq[fi] = sums
    pl.semaphore_wait(barrier, len(greeted))
    for k in range(1, 8):
        send(sq.at[fi], sq.at[fi], sq_s.at[k - 1], sq_r.at[k - 1], peers[k - 1])


    def hrows(m):
        return pl.ds(m * SUB, SUB)

    first_to = (
        jnp.where(inner, cross[0], side[0]),
        jnp.where(inner, cross[1], side[1]),
    )
    first_t = jnp.where(inner, 0, 1)

    def first_send(m):
        send(xv.at[hrows(m)], hid.at[first_t, y, hrows(m)], hx_s.at[0, m], hx_r.at[first_t, m], first_to)

    def own_send(j):
        src = piece(j, own_piece)
        send(src, src, wz_s.at[j, 0, 0], wz_r.at[j, 0, 0], up)
        send(src, src, wz_s.at[j, 1, 0], wz_r.at[j, 1, 0], down)
        send(src, src, ws_s.at[j, 0], ws_r.at[j, 0], sib)

    first_send(0)
    own_send(0)
    first_send(1)
    for j in range(1, BACK[2]):
        own_send(j)
    first_send(2)

    @pl.when(jnp.logical_not(inner))
    def _():
        load_h.wait()

    plan = Plan()
    start = []

    def at(step):
        return ((z + 8 + step) % 8) * 2 + c

    pz, lz = 3.1, 2.0

    def wait_w(j, way, d):
        def go():
            if d < 3:
                ref = piece(j, at(-(d + 1) if way == 0 else d + 1))
            else:
                ref = wts.at[j, pl.ds(pl.multiple_of(at(4) * ROWS + way * 128, 128), 128)]
            remote(ref, ref, wz_s.at[j, way, d], wz_r.at[j, way, d], sib).wait_recv()
        return go

    def wait_s(j, k):
        def go():
            ref = wts.at[j, pl.ds(0, ROWS)]
            remote(ref, ref, ws_s.at[j, k], ws_r.at[j, k], sib).wait_recv()
        return go

    for j in range(NCH):
        for way in range(2):
            for d in range(4):
                plan.token(f"w{j}{way}{d}", wait_w(j, way, d))
        for k in range(8):
            plan.token(f"s{j}{k}", wait_s(j, k))

    def own_task(j):
        plan.add(
            f"own{j}", [f"done:w{j-BACK[0]}{way}{BACK[1]}f" for way in range(2)] if j >= BACK[2] else [], 0.3, 0,
            (lambda: own_send(j)) if j >= BACK[2] else (lambda: None),
            [("zu", pz, lz, f"w{j}00"), ("zd", pz, lz, f"w{j}10"), ("cc", 0.6, 1.0, f"s{j}0")],
        )

    def fwd_task(j, way, d):
        def go():
            idx = at(-(d + 1) if way == 0 else d + 1)
            to = up if way == 0 else down
            if d < 2:
                src = piece(j, idx)
            else:
                src = wts.at[j, pl.ds(pl.multiple_of(idx * ROWS + way * 128, 128), 128)]
            send(src, src, wz_s.at[j, way, d + 1], wz_r.at[j, way, d + 1], to)
            src = piece(j, idx)
            k = 1 + way * 3 + d
            send(src, src, ws_s.at[j, k], ws_r.at[j, k], sib)
        link = "zu" if way == 0 else "zd"
        plan.add(
            f"w{j}{way}{d}f", [f"w{j}{way}{d}"], 0.2, 1, go,
            [(link, pz if d < 2 else pz / 2, lz, f"w{j}{way}{d+1}"), ("cc", 0.6, 1.0, f"s{j}{1+way*3+d}")],
        )

    def last_task(j):
        def go():
            src = piece(j, at(4))
            send(src, src, ws_s.at[j, 7], ws_r.at[j, 7], sib)
        plan.add(f"w{j}l", [f"w{j}03", f"w{j}13"], 0.1, 1, go, [("cc", 0.6, 1.0, f"s{j}7")])

    for j in range(NCH):
        own_task(j)
        for way in range(2):
            for d in range(3):
                fwd_task(j, way, d)
        last_task(j)
    chunk_in = [
        [f"s{j}{k}" for k in range(8)]
        + [f"done:w{j}{way}{d}f" for way in range(2) for d in range(3)]
        + [f"done:w{j}l"]
        for j in range(NCH)
    ]

    ph, lh = 2.35, 2.0

    def hpiece(t, yy, m):
        return hid.at[t, yy, hrows(m)]

    def wait_hx(t, m):
        ref = hpiece(t, y, m)
        remote(ref, ref, hx_s.at[0, m], hx_r.at[t, m], sib).wait_recv()

    def y_sends(t, m):
        ref = hpiece(t, y, m)
        send_when.append(remote(ref, ref, hy_s.at[t, m, 0], hy_r.at[t, m, 0], yup))
        send_when[-1].start()
        send_when.append(remote(ref, ref, hy_s.at[t, m, 1], hy_r.at[t, m, 1], ydown))
        send_when[-1].start()

    send_when = []
    y_links = lambda t, m: [("yu", ph, lh, f"y{t}{m}0"), ("yd", ph, lh, f"y{t}{m}1")]
    seq = [(0, m) for m in range(EARLY)] + [(1, m) for m in range(OWN)] + [(0, m) for m in range(EARLY, NSUB)] + [(1, m) for m in range(OWN, NSUB)]
    rank = {tm: n for n, tm in enumerate(seq)}

    def more(m):
        if m + 3 < NSUB:
            src = xv.at[hrows(m + 3)]
            remote(src, hid.at[first_t, y, hrows(m + 3)], hx_s.at[0, m + 3], hx_r.at[first_t, m + 3], first_to).start()

    def x_in(m):
        def go():
            @pl.when(inner)
            def _():
                wait_hx(0, m)
                ref = hpiece(0, y, m)
                remote(ref, ref, hx_s.at[1, m], hx_r.at[0, m], side).start()
                more(m)
        plan.add(
            f"xi0{m}", [f"xa0{m}"], 0.1, 2, go,
            [("xo", ph, lh, f"xb0{m}")] + ([("xi", ph, lh, f"xa0{m+3}")] if m + 3 < NSUB else []),
        )

    def x_out(m):
        def go():
            @pl.when(jnp.logical_not(inner))
            def _():
                wait_hx(0, m)
                more(m)
        plan.add(
            f"xo0{m}", [f"xb0{m}"], 0.1, 2, go,
            [("xs", ph, lh, f"xc1{m+3}")] if m + 3 < NSUB else [],
        )

    def x_own(m):
        def go():
            @pl.when(inner)
            def _():
                wait_hx(1, m)
        plan.add(f"xo1{m}", [f"xc1{m}"], 0.1, 3, go)

    def y_own(t, m):
        n = rank[(t, m)]
        deps = [f"done:xo{t}{m}"] + ([f"done:xi{t}{m}"] if t == 0 else [])
        if n >= AHEAD:
            deps.append("done:yf%d%d" % seq[n - AHEAD])
        plan.add(f"ys{t}{m}", deps, 0.1, 1.5, lambda: y_sends(t, m), y_links(t, m))

    plan.add(
        "first", [], 0.5, -1, lambda: None,
        [("xi", ph, lh, f"xa0{m}") for m in range(3)] + [("xs", ph, lh, f"xc1{m}") for m in range(3)],
    )
    for m in range(NSUB):
        x_in(m)
        x_out(m)
        x_own(m)
        for t in range(2):
            y_own(t, m)

    def wait_y(t, m, k):
        def go():
            idx = (y + 3) % 4 if k == 0 else (y + 1) % 4 if k == 1 else (y + 2) % 4
            ref = hpiece(t, idx, m)
            remote(ref, ref, hy_s.at[t, m, k], hy_r.at[t, m, k], sib).wait_recv()
        return go

    def y_task(t, m):
        way = m % 2
        for k in range(3):
            plan.token(f"y{t}{m}{k}", wait_y(t, m, k))

        def go():
            ref = hpiece(t, (y + 3) % 4 if way == 0 else (y + 1) % 4, m)
            send(ref, ref, hy_s.at[t, m, 2], hy_r.at[t, m, 2], yup if way == 0 else ydown)
        plan.add(
            f"yf{t}{m}", [f"y{t}{m}{way}"], 0.1, 2, go, [("yu" if way == 0 else "yd", ph, lh, f"y{t}{m}2")]
        )

    def wait_sq(k):
        def go():
            remote(sq.at[0], sq.at[0], sq_s.at[k], sq_r.at[k], sib).wait_recv()
        return go

    def spread(which, rows8):
        inv = lax.rsqrt(rows8 * (1.0 / 8192.0) + 1e-05)
        rs[which] = lax.dot_general(
            inv, jnp.full((8, 128), 0.125, F32), (((0,), (0,)), ((), ())),
            precision=lax.Precision.HIGHEST, preferred_element_type=F32,
        )

    def total():
        rows8 = sq[0]
        for k in range(1, 8):
            rows8 = rows8 + sq[k]
        tot[1] = rows8
        send(tot.at[1], tot.at[0], tx_s.at[0], tx_r.at[0], far)
        spread(1, rows8)

    def wait_tx():
        remote(tot.at[1], tot.at[0], tx_s.at[0], tx_r.at[0], far).wait_recv()

    plan.token("tx", wait_tx)
    for k in range(7):
        start.append(plan.token(f"sq{k}", wait_sq(k)))
    plan.add("sqa", ["done:first"], 3.0, 0, lambda: None)
    plan.add("total", [f"sq{k}" for k in range(7)] + ["done:sqa"], 0.5, 1, total, [("none", 0, 2.5, "tx")])
    plan.add("other", ["tx"], 0.5, 1, lambda: spread(0, tot[0]))

    def norm_task(t, m, step, deps):
        def go():
            yy = (y + step) % 4
            gain = g_ref[pl.ds(xh * 4 + yy, 1), :]
            scale = rs[t, m * SUB:(m + 1) * SUB, :]
            for k in range(WID // 128):
                v = hid[t, yy, m * SUB:(m + 1) * SUB, k * 128:(k + 1) * 128].astype(F32)
                v = v * scale * gain[:, k * 128:(k + 1) * 128]
                nrm[t, m * SUB:(m + 1) * SUB, pl.ds(pl.multiple_of(yy * WID + k * 128, 128), 128)] = v.astype(BF16)
        plan.add(f"n{t}{m}{step}", deps + ["done:other" if t == 0 else "done:total"], 0.05, 4 + rank[(t, m)] * 0.01, go)

    for t in range(2):
        for m in range(NSUB):
            y_task(t, m)
            norm_task(t, m, 0, [f"done:xo{t}{m}"] + ([f"done:xi{t}{m}"] if t == 0 else []))
            norm_task(t, m, 3, [f"y{t}{m}0"])
            norm_task(t, m, 1, [f"y{t}{m}1"])
            norm_task(t, m, 2, [f"y{t}{m}2"])

    def product(t, lo, hi, j):
        return jnp.dot(nrm[t, lo * SUB:hi * SUB, :], wts[j], preferred_element_type=F32)

    def sent(j):
        return TGROUPS[0] if j < 2 else TGROUPS[1]

    def sent_rows(j, h):
        lo, hi = sent(j)[h]
        return pl.ds(lo * SUB, (hi - lo) * SUB)

    def wait_pr(j, h):
        def go():
            ref = got.at[j, sent_rows(j, h)]
            remote(ref, ref, pr_s.at[j, h], pr_r.at[j, h], far).wait_recv()
        return go

    def other_task(h, j):
        lo, hi = sent(j)[h]

        def go():
            rows = sent_rows(j, h)
            part[j, rows] = product(0, lo, hi, j)
            send(part.at[j, rows], got.at[j, rows], pr_s.at[j, h], pr_r.at[j, h], far)
        plan.token(f"p{j}{h}", wait_pr(j, h))
        deps = [f"done:n0{m}{s}" for m in range(lo, hi) for s in range(4)]
        plan.add(
            f"m0{h}{j}", deps + chunk_in[j] + (["done:kb%d" % (len(KGROUPS) - 1)] if j == NCH - 1 else []), 1.0 if hi - lo > 2 else 0.7, 5 + j * 0.1 + h * 0.01, go,
            [("xp", 1.2 * (hi - lo), 3.0, f"p{j}{h}")],
        )

    def rotated(u, rows):
        return u * cosv[rows, :] + pltpu.roll(u, 64, 1) * sinv[rows, :]

    def groups(j):
        return KGROUPS if j == 0 else QGROUPS if j < 3 else ((0, NSUB),)

    def own_product(h, j):
        lo, hi = groups(j)[h]

        def go():
            acc[j, pl.ds(lo * SUB, (hi - lo) * SUB)] = product(1, lo, hi, j)
        deps = [f"done:n1{m}{s}" for m in range(lo, hi) for s in range(4)]
        plan.add(f"m1{h}{j}", deps + chunk_in[j], 1.0 if hi - lo > 2 else 0.7, (4.4 if j == 0 else 6) + j * 0.1 + h * 0.01, go)

    def kv_send(blk_from, blk_to, h, k, to):
        lo, hi = KGROUPS[h]
        rows = pl.ds(lo * SUB, (hi - lo) * SUB)
        send(kvb.at[blk_from, rows], kvb.at[blk_to, rows], kv_s.at[k, h], kv_r.at[k, h], to)

    def kv_time(h):
        return 0.55 * (KGROUPS[h][1] - KGROUPS[h][0])

    def finish(h, j):
        lo, hi = groups(j)[h]

        def go():
            rows = pl.ds(lo * SUB, (hi - lo) * SUB)
            u = acc[j, rows] + got[j, rows]
            left, right = u[:, :HD], u[:, HD:]
            if j == 0:
                kvb[4 + c, rows, 0:HD] = rotated(left, rows).astype(BF16)
                kvb[4 + c, rows, HD:2 * HD] = right.astype(BF16)
                kv_send(4 + c, 2 + c, h, 0, after)
                kv_send(4 + c, 4 + c, h, 2, sib)
            else:
                qbuf[j - 1, rows, 0:HD] = rotated(left, rows).astype(BF16)
                qbuf[j - 1, rows, HD:2 * HD] = rotated(right, rows).astype(BF16)
        sends = [("zu", kv_time(h), 2.0, f"k0{h}"), ("cc", 0.3, 1.0, f"k2{h}")] if j == 0 else []
        parts = [p for p, (a, b) in enumerate(sent(j)) if a < hi and b > lo]
        plan.add(
            f"f{h}{j}", [f"done:m1{h}{j}", "done:rope"] + [f"p{j}{p}" for p in parts], 0.2, 4.5 + j * 0.1, go, sends
        )

    def rope():
        load_c.wait()
        load_n.wait()
        cosv[...] = jnp.concatenate([half_c[...], half_c[...]], axis=1)
        sinv[...] = jnp.concatenate([-half_n[...], half_n[...]], axis=1)

    plan.add("rope", ["done:other"], 0.5, 3.5, rope)

    def wait_kv(k, h):
        def go():
            ref = kvb.at[0, pl.ds(0, (KGROUPS[h][1] - KGROUPS[h][0]) * SUB)]
            remote(ref, ref, kv_s.at[k, h], kv_r.at[k, h], sib).wait_recv()
        return go

    for h in range(len(KGROUPS)):
        for k in range(5):
            plan.token(f"k{k}{h}", wait_kv(k, h))

        def pass_one(h=h):
            kv_send(2 + c, c, h, 1, after)
            kv_send(2 + c, 2 + c, h, 3, sib)

        def pass_two(h=h):
            kv_send(c, c, h, 4, sib)

        plan.add(f"ka{h}", [f"k0{h}"], 0.1, 1, pass_one, [("zu", kv_time(h), 2.0, f"k1{h}"), ("cc", 0.3, 1.0, f"k3{h}")])
        plan.add(f"kb{h}", [f"k1{h}"], 0.1, 1, pass_two, [("cc", 0.3, 1.0, f"k4{h}")])
    for j in range(NCH):
        for h in range(len(sent(j))):
            other_task(h, j)
        for h in range(len(groups(j))):
            own_product(h, j)
            finish(h, j)
    ngk = len(KGROUPS)
    window_in = [f"k{k}{h}" for k in (2, 3, 4) for h in range(ngk)] + [f"done:kb{h}" for h in range(ngk)] + [f"done:f{h}0" for h in range(ngk)]

    def attend(j):
        def go():
            row = lax.broadcasted_iota(jnp.int32, (2 * HD, HD), 0)
            col = lax.broadcasted_iota(jnp.int32, (2 * HD, HD), 1)
            later = col > row % HD
            key_at = lax.broadcasted_iota(jnp.int32, (1, WIN), 1)

            def block(b, carry):
                r0 = pl.multiple_of(b * HD, HD)
                k0 = pl.multiple_of(c * TOK + b * HD, HD)
                keys = kvf[pl.ds(k0, WIN), 0:HD]
                vals = kvf[pl.ds(k0, WIN), HD:2 * HD]
                real = key_at >= (STEPS - ci) * TOK - b * HD
                q = jnp.concatenate(
                    [qbuf[j - 1, pl.ds(r0, HD), 0:HD], qbuf[j - 1, pl.ds(r0, HD), HD:2 * HD]], axis=0
                )
                s = lax.dot_general(q, keys, (((1,), (1,)), ((), ())), preferred_element_type=F32)
                s = jnp.concatenate(
                    [
                        jnp.where(later, s[:, :HD], NEG),
                        s[:, HD:WIN - HD],
                        jnp.where(later, NEG, s[:, WIN - HD:]),
                    ],
                    axis=1,
                )
                s = jnp.where(real, s, NEG)
                peak = jnp.max(s, axis=1, keepdims=True)
                e = jnp.exp2((s - peak) * EXP_SCALE)
                probs = (e * (1.0 / jnp.sum(e, axis=1, keepdims=True))).astype(BF16)
                o = jnp.dot(probs, vals, preferred_element_type=F32).astype(BF16)
                o_ref[pl.ds(r0, HD), (j - 1) * 256:(j - 1) * 256 + HD] = o[:HD]
                o_ref[pl.ds(r0, HD), (j - 1) * 256 + HD:j * 256] = o[HD:]
                return carry

            lax.fori_loop(0, TOK // HD, block, 0, unroll=True)
        plan.add(f"a{j}", window_in + [f"done:f{h}{j}" for h in range(len(groups(j)))], 3.0, 7 + j, go)

    kvf = kvb.reshape(6 * TOK, 2 * HD)
    for j in range(1, NCH):
        attend(j)

    plan.emit(start)
    body.total = plan.total

    for cp in started:
        cp.wait_send()
    for t in range(2):
        for m in range(NSUB):
            for k in range(2):
                ref = hpiece(t, y, m)
                remote(ref, ref, hy_s.at[t, m, k], hy_r.at[t, m, k], yup).wait_send()

    for m in range(3, NSUB):
        remote(xv.at[hrows(m)], hid.at[first_t, y, hrows(m)], hx_s.at[0, m], hx_r.at[first_t, m], first_to).wait_send()

    @pl.when(inner)
    def _():
        for m in range(NSUB):
            ref = hpiece(0, y, m)
            remote(ref, ref, hx_s.at[1, m], hx_r.at[0, m], side).wait_send()


def shards(hidden_states, norm_gain, qkv_weight, block_mask):
    ci = lax.axis_index("ctx")
    position = (ci * TOK + jnp.arange(TOK, dtype=jnp.int32)).astype(F32)
    inverse = jnp.power(F32(500000.0), -(jnp.arange(0, HD, 2).astype(F32) / HD))
    angles = position[:, None] * inverse[None, :]
    cosine, sine = jnp.cos(angles), jnp.sin(angles)
    gain = norm_gain.astype(F32).reshape(8, WID)
    any_ = pl.BlockSpec(memory_space=pl.ANY)
    hbm = pl.BlockSpec(memory_space=pltpu.HBM)
    dma = pltpu.SemaphoreType.DMA
    result = pl.pallas_call(
        body,
        out_shape=jax.ShapeDtypeStruct((TOK, 1024), BF16),
        in_specs=[
            hbm, pl.BlockSpec(memory_space=pltpu.VMEM), hbm, pl.BlockSpec(memory_space=pltpu.SMEM), any_, any_,
        ],
        out_specs=pl.BlockSpec(memory_space=pltpu.VMEM),
        scratch_shapes=[
            pltpu.VMEM((TOK, WID), BF16),
            pltpu.VMEM((ROWS, 1280), BF16),
            pltpu.VMEM((TOK, HD // 2), F32),
            pltpu.VMEM((TOK, HD // 2), F32),
            pltpu.VMEM((TOK, HD), F32),
            pltpu.VMEM((TOK, HD), F32),
            pltpu.VMEM((2, 4, TOK, WID), BF16),
            pltpu.VMEM((2, TOK, KH), BF16),
            pltpu.VMEM((NCH, KH, 256), BF16),
            pltpu.VMEM((NCH, TOK, 256), F32),
            pltpu.VMEM((NCH, TOK, 256), F32),
            pltpu.VMEM((NCH, TOK, 256), F32),
            pltpu.VMEM((4, TOK, 256), BF16),
            pltpu.VMEM((6, TOK, 256), BF16),
            pltpu.VMEM((8, 8, TOK), F32),
            pltpu.VMEM((2, 8, TOK), F32),
            pltpu.VMEM((2, TOK, HD), F32),
            dma((5,)),
            dma((NCH, 2, 4)), dma((NCH, 2, 4)),
            dma((NCH, 8)), dma((NCH, 8)),
            dma((2, NSUB)), dma((2, NSUB)),
            dma((2, NSUB, 3)), dma((2, NSUB, 3)),
            dma((7,)), dma((7,)),
            dma((1,)), dma((1,)),
            dma((NCH, 4)), dma((NCH, 4)),
            dma((5, len(KGROUPS))), dma((5, len(KGROUPS))),
        ],
        compiler_params=pltpu.CompilerParams(
            collective_id=0, has_side_effects=True, vmem_limit_bytes=52 * 2**20
        ),
        cost_estimate=pl.CostEstimate(flops=12 * 10**9, bytes_accessed=3 * 10**6, transcendentals=6 * 10**6),
    )(
        hidden_states, gain, qkv_weight.reshape(ROWS, 1280), block_mask.reshape(2, 10), cosine, sine,
    )
    return result.reshape(TOK, 1, 1024)


def solution(mesh):
    return jax.shard_map(
        shards,
        mesh=mesh,
        in_specs=(P("ctx", "fsdp"), P(), P("ctx", "fsdp", None), P("ctx", "fsdp", None)),
        out_specs=P("ctx", "fsdp", None),
        check_vma=False,
    )
```
